128 devices in a mesh: lon: 32 (over y, x_hi, z), lat: 4 (over x_lo, core).
Axes of the slice: x: 4 (x_hi: 2, x_lo: 2; x = x_hi * 2 + x_lo), y: 4, z: 4, core: 2. Of those that a mesh axis runs over, the one named last changes fastest.
Arguments:
- field: bfloat16 [8, 24, 73728], P(None, 'lat', 'lon'), may hold values from -6 to 6
- cotangent: bfloat16 [8, 24, 73728], P(None, 'lat', 'lon'), may hold values from -6 to 6
- gain_attn: float32 [192], replicated, may hold values from 0.25 to 1.75
- gain_mlp: float32 [192], replicated, may hold values from 0.25 to 1.75
- qkv_weight: bfloat16 [192, 576], replicated, may hold values from -0.4375 to 0.4375
- proj_weight: bfloat16 [192, 192], replicated, may hold values from -0.4375 to 0.4375
- fc1_weight: bfloat16 [192, 768], replicated, may hold values from -0.4375 to 0.4375
- fc2_weight: bfloat16 [768, 192], replicated, may hold values from -0.21875 to 0.21875
- bias_table: float32 [4, 4, 6, 23, 144], P(None, 'lat'), may hold values from -5 to 400
Outputs:
- mixed: bfloat16 [8, 24, 73728], P(None, 'lat', 'lon')
- field_grad: bfloat16 [8, 24, 73728], P(None, 'lat', 'lon')
- qkv_grad: float32 [192, 576], replicated
- proj_grad: float32 [192, 192], replicated
- fc1_grad: float32 [192, 768], replicated
- fc2_grad: float32 [768, 192], replicated
- gain_attn_grad: float32 [192], replicated
- gain_mlp_grad: float32 [192], replicated
- table_grad: float32 [4, 4, 6, 23, 144], P(None, 'lat')
The draws below stay inside these ranges and needn't reach their ends.
All inputs are finite; a program needn't handle non-finite values.
Results may differ from the reference program's by a relative error of at most 0.034.
Values may be sent and summed in bfloat16 or wider, within the bound.
A program may use at most 192 MiB of HBM per device.

```python
import jax
import jax.numpy as jnp
from jax import lax

C = 192
HEADS = 6
HIDDEN_SIZE = 768
WIN_Z = 2
WIN_LAT = 6
WIN_LON = 12
LEVELS = 8
NLAT = 24
NLON = 384
NZW = 4
NLATW = 4


def draw_bias_table(key, part):
    key = jax.random.fold_in(key, 7)
    pair_count = WIN_Z * WIN_Z * WIN_LAT * WIN_LAT
    rel_count = 2 * WIN_LON - 1
    draw_shape = (NZW, NLATW, HEADS, rel_count, pair_count)
    base_key = jax.random.fold_in(key, 0)
    values = jax.random.truncated_normal(base_key, -5.0, 5.0, draw_shape, jnp.float32)
    return values.astype(jnp.float32)


def block_levels(key, extent, cuts, smallest, largest):
    loudness, own = 1.0, jax.random.fold_in(key, 6)
    for axis_at, shards_of in cuts:
        draws = jnp.exp(jax.random.uniform(jax.random.fold_in(own, axis_at), (shards_of,), jnp.float32, smallest / len(cuts), largest / len(cuts)))
        loudness = loudness * jnp.repeat(draws, extent[axis_at] // shards_of).reshape([-1 if axis == axis_at else 1 for axis in range(len(extent))])
    return loudness


def noise(rng, extent, scale, bound, cuts=(), dtype=jnp.bfloat16):
    entries = scale * jax.random.normal(rng, extent, jnp.float32)
    if cuts:
        entries = entries * block_levels(rng, extent, cuts, -0.22, 0.18)
    return jnp.clip(entries, -bound, bound).astype(dtype)


def setup_inputs(seed: int = 0) -> dict:
    splits = jax.random.split(jax.random.key(seed), 10)
    return {
        "field": noise(splits[0], (LEVELS, NLAT, NLON * C), 1.0, 6.0, ((1, 4), (2, 32))),
        "cotangent": noise(splits[1], (LEVELS, NLAT, NLON * C), 1.0, 6.0, ((1, 4), (2, 32))),
        "gain_attn": jnp.clip(1.0 + 0.15 * jax.random.normal(splits[2], (C,), jnp.float32), 0.25, 1.75),
        "gain_mlp": jnp.clip(1.0 + 0.15 * jax.random.normal(splits[3], (C,), jnp.float32), 0.25, 1.75),
        "qkv_weight": noise(splits[4], (C, 3 * C), C ** -0.5, 0.4375),
        "proj_weight": noise(splits[5], (C, C), C ** -0.5, 0.4375),
        "fc1_weight": noise(splits[6], (C, HIDDEN_SIZE), C ** -0.5, 0.4375),
        "fc2_weight": noise(splits[7], (HIDDEN_SIZE, C), HIDDEN_SIZE ** -0.5, 0.21875),
        "bias_table": draw_bias_table(jax.random.fold_in(splits[9], 71), 0),
    }


EPSILON = 1e-05
MASKED = -1000000000.0

def product_of(form, left, right):
    return jnp.einsum(form, left.astype(jnp.float32), right.astype(jnp.float32), precision=lax.Precision.HIGHEST)

def norm_scale(values, gain):
    centre = values - lax.optimization_barrier(jnp.mean(values, axis=-1, keepdims=True))
    spread = lax.optimization_barrier(jnp.mean(centre * centre, axis=-1, keepdims=True))
    return centre * lax.rsqrt(spread + EPSILON) * gain

def gelu_tanh(values):
    return jax.nn.gelu(values, approximate=True)

def to_windows(tile, channels):
    level_count, row_count, flat = tile.shape
    col_count = flat // channels
    shaped = tile.reshape(level_count // WIN_Z, WIN_Z, row_count // WIN_LAT, WIN_LAT, col_count // WIN_LON, WIN_LON, channels)
    shaped = shaped.transpose(0, 2, 4, 1, 3, 5, 6)
    return shaped.reshape(level_count // WIN_Z, row_count // WIN_LAT, col_count // WIN_LON, WIN_Z * WIN_LAT * WIN_LON, channels)

def from_windows(windows):
    z_windows, a_windows, l_windows, tokens_win, channels = windows.shape
    shaped = windows.reshape(z_windows, a_windows, l_windows, WIN_Z, WIN_LAT, WIN_LON, channels)
    shaped = shaped.transpose(0, 3, 1, 4, 2, 5, 6)
    return shaped.reshape(z_windows * WIN_Z, a_windows * WIN_LAT, l_windows * WIN_LON * channels)

def regions(z_windows, a_windows, first_window, total_windows):
    level_in = jnp.arange(WIN_Z)[None, None, :, None, None]
    row_in = jnp.arange(WIN_LAT)[None, None, None, :, None]
    level_last = (jnp.arange(z_windows) == z_windows - 1)[:, None, None, None, None]
    row_last = (jnp.arange(a_windows) + first_window == total_windows - 1)[None, :, None, None, None]
    level_label = jnp.logical_and(level_last, level_in == WIN_Z - 1).astype(jnp.int32)
    row_label = jnp.logical_and(row_last, row_in >= WIN_LAT - WIN_LAT // 2).astype(jnp.int32)
    labels = jnp.broadcast_to(2 * level_label + row_label, (z_windows, a_windows, WIN_Z, WIN_LAT, WIN_LON))
    return labels.reshape(z_windows, a_windows, WIN_Z * WIN_LAT * WIN_LON)

def offset_table(rel_count):
    places = jnp.arange(WIN_LON)
    distance = places[:, None] - places[None, :] + WIN_LON - 1
    onehot = (distance[None, :, :] == jnp.arange(rel_count)[:, None, None]).astype(jnp.float32)
    return onehot.reshape(rel_count, WIN_LON * WIN_LON)

def expand_bias(table, labels):
    z_windows, a_windows, head_count, rel_count, pair_count = table.shape
    tokens_win = WIN_Z * WIN_LAT * WIN_LON
    spread = jnp.einsum('abhrm,rn->abhmn', table, offset_table(rel_count), precision=lax.Precision.HIGHEST)
    spread = spread.reshape(z_windows, a_windows, head_count, WIN_Z, WIN_Z, WIN_LAT, WIN_LAT, WIN_LON, WIN_LON)
    spread = spread.transpose(0, 1, 2, 3, 5, 7, 4, 6, 8).reshape(z_windows, a_windows, head_count, tokens_win, tokens_win)
    allowed = labels[:, :, None, :, None] == labels[:, :, None, None, :]
    return jnp.where(allowed, spread, MASKED)

def shrink_bias(d_bias, rel_count):
    z_windows, a_windows, head_count, tokens_win, tokens_other = d_bias.shape
    shaped = d_bias.reshape(z_windows, a_windows, head_count, WIN_Z, WIN_LAT, WIN_LON, WIN_Z, WIN_LAT, WIN_LON)
    shaped = shaped.transpose(0, 1, 2, 3, 6, 4, 7, 5, 8).reshape(z_windows, a_windows, head_count, WIN_Z * WIN_Z * WIN_LAT * WIN_LAT, WIN_LON * WIN_LON)
    return jnp.einsum('abhmn,rn->abhrm', shaped, offset_table(rel_count), precision=lax.Precision.HIGHEST)

def attend(windows, qkv_weight, proj_weight, bias_full):
    z_windows, a_windows, l_windows, tokens_win, channels = windows.shape
    head_count = bias_full.shape[2]
    head_size = channels // head_count
    scaling = head_size ** (-0.5)
    projected = product_of('abltc,cd->abltd', windows, qkv_weight)
    projected = projected.reshape(z_windows, a_windows, l_windows, tokens_win, 3, head_count, head_size)
    queries = (projected[:, :, :, :, 0] * scaling).astype(jnp.bfloat16)
    key_part = projected[:, :, :, :, 1].astype(jnp.bfloat16)
    value_part = projected[:, :, :, :, 2].astype(jnp.bfloat16)
    scores = product_of('abltho,ablsho->ablhts', queries, key_part) + bias_full[:, :, None]
    row_top = lax.optimization_barrier(jnp.max(scores, axis=-1, keepdims=True))
    raised = jnp.exp(scores - row_top)
    softmaxed = raised / lax.optimization_barrier(jnp.sum(raised, axis=-1, keepdims=True))
    context = product_of('ablhts,ablsho->abltho', softmaxed.astype(jnp.bfloat16), value_part).astype(jnp.bfloat16)
    context = context.reshape(z_windows, a_windows, l_windows, tokens_win, channels)
    attended = product_of('abltc,cd->abltd', context, proj_weight).astype(jnp.bfloat16)
    return (attended, (queries, key_part, value_part, softmaxed, context))

def attend_back(windows, d_attended, saved, qkv_weight, proj_weight):
    queries, key_part, value_part, softmaxed, context = saved
    z_windows, a_windows, l_windows, tokens_win, channels = windows.shape
    head_count = queries.shape[4]
    head_size = queries.shape[5]
    scaling = head_size ** (-0.5)
    d_proj = product_of('abltc,abltd->cd', context, d_attended)
    d_context = product_of('abltd,cd->abltc', d_attended, proj_weight).astype(jnp.bfloat16)
    d_context = d_context.reshape(z_windows, a_windows, l_windows, tokens_win, head_count, head_size)
    d_probs = product_of('abltho,ablsho->ablhts', d_context, value_part)
    d_values = product_of('ablhts,abltho->ablsho', softmaxed.astype(jnp.bfloat16), d_context)
    d_scores = softmaxed * (d_probs - lax.optimization_barrier(jnp.sum(d_probs * softmaxed, axis=-1, keepdims=True)))
    d_bias = lax.optimization_barrier(jnp.sum(d_scores, axis=2))
    d_low = d_scores.astype(jnp.bfloat16)
    d_queries = product_of('ablhts,ablsho->abltho', d_low, key_part) * scaling
    d_keys = product_of('ablhts,abltho->ablsho', d_low, queries)
    d_projected = jnp.stack([d_queries, d_keys, d_values], axis=4)
    d_projected = d_projected.reshape(z_windows, a_windows, l_windows, tokens_win, 3 * channels).astype(jnp.bfloat16)
    d_qkv = product_of('abltc,abltd->cd', windows, d_projected)
    d_windows = product_of('abltd,cd->abltc', d_projected, qkv_weight).astype(jnp.bfloat16)
    return (d_windows, d_qkv, d_proj, d_bias)

def mlp_pass(field_wide, attn_back, cotangent, gain_mlp, fc1_weight, fc2_weight):
    channels = gain_mlp.shape[0]
    contract_rows = (((0,), (0,)), ((), ()))
    contract_cols = (((1,), (1,)), ((), ()))
    resid = field_wide + attn_back.astype(jnp.float32)
    normed, norm_back = jax.vjp(norm_scale, resid, gain_mlp)
    normed_low = normed.astype(jnp.bfloat16).reshape(-1, channels)
    hidden_pre = jnp.dot(normed_low, fc1_weight, preferred_element_type=jnp.float32)
    activated, gelu_back = jax.vjp(gelu_tanh, hidden_pre)
    hidden_low = activated.astype(jnp.bfloat16)
    output = jnp.dot(hidden_low, fc2_weight, preferred_element_type=jnp.float32).reshape(resid.shape)
    mixed = (resid + output).astype(jnp.bfloat16)
    flat_cot = cotangent.reshape(-1, channels)
    d_fc2 = lax.dot_general(hidden_low, flat_cot, contract_rows, preferred_element_type=jnp.float32)
    d_hidden = lax.dot_general(flat_cot, fc2_weight, contract_cols, preferred_element_type=jnp.float32).astype(jnp.bfloat16)
    d_pre = gelu_back(d_hidden.astype(jnp.float32))[0].astype(jnp.bfloat16)
    d_fc1 = lax.dot_general(normed_low, d_pre, contract_rows, preferred_element_type=jnp.float32)
    d_normed = lax.dot_general(d_pre, fc1_weight, contract_cols, preferred_element_type=jnp.float32).reshape(resid.shape)
    d_resid_norm, d_gain_mlp = norm_back(d_normed)
    d_resid = cotangent.astype(jnp.float32) + d_resid_norm
    return (mixed, d_resid, d_fc1, d_fc2, d_gain_mlp)

def reference(field, cotangent, gain_attn, gain_mlp, qkv_weight, proj_weight, fc1_weight, fc2_weight, bias_table):
    channels = gain_attn.shape[0]
    level_count, row_count, flat = field.shape
    col_count = flat // channels
    grid_shape = (level_count, row_count, col_count, channels)
    lead_steps = (-1, -(WIN_LAT // 2), -(WIN_LON // 2) * channels)
    trail_steps = (1, WIN_LAT // 2, WIN_LON // 2 * channels)
    field_wide = field.astype(jnp.float32).reshape(grid_shape)
    normed, norm_back = jax.vjp(norm_scale, field_wide, gain_attn)
    normed_low = normed.astype(jnp.bfloat16).reshape(level_count, row_count, flat)
    shifted = jnp.roll(normed_low, lead_steps, axis=(0, 1, 2))
    windows = to_windows(shifted, channels)
    labels = regions(windows.shape[0], windows.shape[1], 0, windows.shape[1])
    bias_full = expand_bias(bias_table, labels)
    columns = jnp.moveaxis(windows, 2, 0)[:, :, :, None]

    def forward_column(column):
        return attend(column, qkv_weight, proj_weight, bias_full)[0]
    attended = jnp.moveaxis(lax.map(forward_column, columns)[:, :, :, 0], 0, 2)
    attn_back = jnp.roll(from_windows(attended), trail_steps, axis=(0, 1, 2))

    def level_pass(items):
        return mlp_pass(items[0], items[1], items[2], gain_mlp, fc1_weight, fc2_weight)
    mixed, d_resid, d_fc1_all, d_fc2_all, d_gain_all = lax.map(level_pass, (field_wide, attn_back.reshape(grid_shape), cotangent.reshape(grid_shape)))
    d_shifted_out = jnp.roll(d_resid.astype(jnp.bfloat16).reshape(level_count, row_count, flat), lead_steps, axis=(0, 1, 2))
    d_columns = jnp.moveaxis(to_windows(d_shifted_out, channels), 2, 0)[:, :, :, None]

    def backward_column(carry, items):
        column, d_column = items
        attended_col, saved = attend(column, qkv_weight, proj_weight, bias_full)
        d_windows, d_qkv, d_proj, d_bias = attend_back(column, d_column, saved, qkv_weight, proj_weight)
        return ((carry[0] + d_qkv, carry[1] + d_proj, carry[2] + d_bias), d_windows)
    start = (jnp.zeros(qkv_weight.shape, jnp.float32), jnp.zeros(proj_weight.shape, jnp.float32), jnp.zeros(bias_full.shape, jnp.float32))
    totals, d_cols = lax.scan(backward_column, start, (columns, d_columns))
    d_windows = jnp.moveaxis(d_cols[:, :, :, 0], 0, 2)
    d_normed = jnp.roll(from_windows(d_windows), trail_steps, axis=(0, 1, 2))
    d_field_norm, d_gain_attn = norm_back(d_normed.reshape(grid_shape).astype(jnp.float32))
    field_grad = (d_resid + d_field_norm).astype(jnp.bfloat16).reshape(level_count, row_count, flat)
    table_grad = shrink_bias(totals[2], bias_table.shape[3])
    return (mixed.reshape(level_count, row_count, flat), field_grad, totals[0], totals[1], lax.optimization_barrier(jnp.sum(d_fc1_all, axis=0)), lax.optimization_barrier(jnp.sum(d_fc2_all, axis=0)), d_gain_attn, lax.optimization_barrier(jnp.sum(d_gain_all, axis=0)), table_grad)
```

```python
import functools
import jax
import jax.numpy as jnp
import numpy as np
from jax import lax
from jax.experimental import pallas as pl
from jax.experimental.pallas import tpu as pltpu
from jax.sharding import PartitionSpec as P

BF = jnp.bfloat16
F32 = jnp.float32
C = 192
HEADS = 6
HEAD = 32
HID = 768
WZ, WR, WC = 2, 6, 12
A = WZ * WR
TW = A * WC
NW = 4
TOK = NW * TW
REL = 2 * WC - 1
RELP = 24
HT = HEADS * TW
ZL = REL * HEADS * A
EPS = 1e-05
MASKED = -1000000000.0


def constants():
    perm = np.zeros((WC, 8, 8, NW, WC, WZ, WR), np.float32)
    for c in range(WC):
        for w in range(NW):
            for lev in range(WZ):
                for r in range(WR):
                    perm[c, (2 * w + lev + 1) % 8, r, w, c, lev, r] = 1
    perm = perm.reshape(WC * 64, TOK)
    expand = np.zeros((WC, A, WC, HEADS, A), np.float32)
    for c in range(WC):
        for a in range(A):
            expand[c, a, c, :, a] = 1
    expand = expand.reshape(TW, HT)
    head_mask = np.zeros((HEADS, HEAD, WC, HEADS, A), np.float32)
    for h in range(HEADS):
        head_mask[h, :, :, h, :] = 1
    head_mask = head_mask.reshape(C, HT)
    rep = np.zeros((HEADS, RELP, REL, HEADS, A), np.float32)
    for h in range(HEADS):
        for rel in range(REL):
            rep[h, rel, rel, h, :] = 1
    rep = rep.reshape(HEADS * RELP, ZL)
    pair = np.zeros((WZ, WZ, WR, WR, WZ, WR, 16), np.float32)
    for lt in range(WZ):
        for ls in range(WZ):
            for rt in range(WR):
                for rs in range(WR):
                    pair[lt, ls, rt, rs, lt, rt, ls * WR + rs] = 1
    pair = pair.reshape(TW, A * 16)
    lane_a = np.arange(ZL) % A
    entry = (np.arange(A)[:, None] == lane_a[None, :]).astype(np.float32)
    entry = np.concatenate([entry, np.zeros((4, ZL), np.float32)])
    b = np.arange(16)
    level_differs = ((b[:, None] // WR) != (lane_a[None, :] // WR)) & (b[:, None] < A)
    row_differs = ((b[:, None] % WR >= 3) != (lane_a[None, :] % WR >= 3)) & (b[:, None] < A)
    differs = np.stack([level_differs, row_differs]).astype(np.float32)
    return [np.asarray(v, dtype=BF) for v in (perm, expand, head_mask, rep, pair)] + [entry, differs]


def nn(a, b):
    return lax.dot_general(a, b, (((1,), (0,)), ((), ())), preferred_element_type=F32)


def nt(a, b):
    return lax.dot_general(a, b, (((1,), (1,)), ((), ())), preferred_element_type=F32)


def tn(a, b):
    return lax.dot_general(a, b, (((0,), (0,)), ((), ())), preferred_element_type=F32)


def column_of(row):
    size = row.shape[1]
    eye = lax.broadcasted_iota(jnp.int32, (size, size), 0) == lax.broadcasted_iota(jnp.int32, (size, size), 1)
    return jnp.sum(jnp.where(eye, row, 0.0), axis=1, keepdims=True)


def row_of(column):
    size = column.shape[0]
    eye = lax.broadcasted_iota(jnp.int32, (size, size), 0) == lax.broadcasted_iota(jnp.int32, (size, size), 1)
    return jnp.sum(jnp.where(eye, column, 0.0), axis=0, keepdims=True)


def normalise(v):
    centre = v - jnp.sum(v, axis=0, keepdims=True) * (1.0 / C)
    inv = lax.rsqrt(jnp.sum(centre * centre, axis=0, keepdims=True) * (1.0 / C) + EPS)
    return centre * inv, inv


def normalise_back(g, hat, inv):
    return inv * (g - jnp.sum(g, axis=0, keepdims=True) * (1.0 / C) - hat * (jnp.sum(g * hat, axis=0, keepdims=True) * (1.0 / C)))


def gather_tokens(x_ref, own, lon, lat, diag):
    for c in range(WC):
        at = slice(c % 6 * C, (c % 6 + 1) * C)
        top, low = (own, lat) if c < 6 else (lon, diag)
        x_ref[c, :, 0:3, :] = top[:, :, at].astype(F32)[:, 3:6, :]
        x_ref[c, :, 3:6, :] = low[:, :, at].astype(F32)[:, 0:3, :]


HALF = WC * C // 2
LANES = 128
PEERS = 16
ROWS = (80, 32)
TROWS = 48
MESH_ID = pl.DeviceIdType.MESH


def place():
    lon, lat = lax.axis_index("lon"), lax.axis_index("lat")
    z, xh, y = lon % 4, (lon // 4) % 2, lon // 8
    return lon, lat, y * 4 + z, xh, xh * 2 + lat // 2, lat % 2


def plane_id(p, xh, lat):
    return ((p // 4) * 8 + xh * 4 + p % 4, lat)


def column_id(t, me, core):
    return ((me // 4) * 8 + (t // 2) * 4 + me % 4, (t % 2) * 2 + core)


def remote(src, dst, sends, recvs, k, device):
    return pltpu.make_async_remote_copy(
        src_ref=src, dst_ref=dst, send_sem=sends.at[k], recv_sem=recvs.at[k], device_id=device, device_id_type=MESH_ID
    )


def total(ref, count):
    value = ref[0].astype(F32)
    for k in range(1, count):
        value = value + ref[k].astype(F32)
    return value.astype(BF)


class PlaneSum:
    def __init__(self, piece, terms, part, cross, final, plane_sems, x_sems, back_sems, local_sem, table):
        self.piece, self.terms, self.part, self.cross, self.final = piece, terms, part, cross, final
        self.plane_sems, self.x_sems, self.back_sems, self.local_sem, self.table = plane_sems, x_sems, back_sems, local_sem, table
        self.lon, self.lat, self.me, self.xh, self.xi, self.core = place()

    def start(self):
        self.copies = []
        for s in range(1, PEERS):
            p = (self.me + s) % PEERS
            copy = remote(self.piece(p), self.terms.at[s], *self.plane_sems, s, plane_id(p, self.xh, self.lat))
            copy.start()
            self.copies.append(copy)

    def across(self):
        self.terms[0] = self.piece(self.me)[...]
        for copy in self.copies:
            copy.wait()
        value = total(self.terms, PEERS)
        self.part[...] = value
        count = 2 if self.table else 4
        mine = self.xh if self.table else self.xi
        self.cross[mine] = value
        self.copies = []
        for s in range(1, count):
            t = (mine + s) % count
            device = ((self.me // 4) * 8 + t * 4 + self.me % 4, self.lat) if self.table else column_id(t, self.me, self.core)
            copy = remote(self.part, self.cross.at[mine], *self.x_sems, s, device)
            copy.start()
            self.copies.append(copy)

    def back(self):
        for copy in self.copies:
            copy.wait()
        self.part[...] = total(self.cross, 2 if self.table else 4)
        self.own = pltpu.make_async_copy(self.part, self.final(self.me), self.local_sem)
        self.own.start()
        self.copies = []
        for s in range(1, PEERS):
            p = (self.me + s) % PEERS
            copy = remote(self.part, self.final(self.me), *self.back_sems, s, plane_id(p, self.xh, self.lat))
            copy.start()
            self.copies.append(copy)

    def finish(self):
        self.own.wait()
        for copy in self.copies:
            copy.wait()


class CoreSum(PlaneSum):
    def __init__(self, grads, got, halves, final, core_sems, rows, *args):
        self.grads, self.got, self.halves, self.whole, self.core_sems, self.rows = grads, got, halves, final, core_sems, rows
        core = lax.axis_index("lat") % 2
        super().__init__(lambda p: halves.at[p], args[0], args[1], args[2], lambda p: final.at[core * PEERS + p], *args[3:], False)

    def start_core(self):
        other = (self.lon, self.lat // 2 * 2 + 1 - self.core)
        self.swap = remote(self.grads.at[pl.ds((1 - self.core) * PEERS, PEERS)], self.got, *self.core_sems, 0, other)
        self.swap.start()

    def start(self):
        self.swap.wait()
        for p in range(PEERS):
            self.halves[p] = (self.grads[self.core * PEERS + p].astype(F32) + self.got[p].astype(F32)).astype(BF)
        super().start()

    def finish(self):
        super().finish()
        other = (self.lon, self.lat // 2 * 2 + 1 - self.core)
        mine = self.whole.at[pl.ds(self.core * PEERS, PEERS)]
        self.swap = remote(mine, mine, *self.core_sems, 1, other)
        self.swap.start()

    def finish_core(self):
        self.swap.wait()


def put_tiles(ref, rows, first, value):
    done = 0
    while done < value.shape[0]:
        piece, row = divmod(first + done, rows)
        count = min(rows - row, value.shape[0] - done)
        ref[piece, row:row + count, :] = value[done:done + count]
        done += count


def get_tiles(ref, rows, first, count):
    parts, done = [], 0
    while done < count:
        piece, row = divmod(first + done, rows)
        take = min(rows - row, count - done)
        parts.append(ref[piece, row:row + take, :].astype(F32))
        done += take
    return parts[0] if len(parts) == 1 else jnp.concatenate(parts, axis=0)


def block_kernel(
    field_ref, cot_ref, gain_attn, gain_mlp, qkv_w, proj_w, fc1_w, fc2_w, table,
    perm, expand, head_mask, rep, pair, entry, differs,
    mixed_own, mixed_got, fgrad_own, fgrad_got, final0, final1, final_t,
    x_ref, t_ref, bias_ref, z_ref, p_ref, qblk_ref, q_ref, k_ref, v_ref, kv_ref, ctx_ref, dctx_ref, dproj_ref,
    halo_ref, send_ref, grads0, grads1, grads_t, got0, got1, halves0, halves1,
    terms0, terms1, terms_t, part0, part1, part_t, cross0, cross1, cross_t,
    local_sems, halo_send, halo_recv, trail_send, trail_recv, core_send, core_recv,
    plane_send, plane_recv, x_send, x_recv, back_send, back_recv,
):
    lon, lat, me, xh, xi, core = place()
    lon_n, lat_n = 32, 4
    west, east = (lon + lon_n - 1) % lon_n, (lon + 1) % lon_n
    above, below = (lat + lat_n - 1) % lat_n, (lat + 1) % lat_n

    barrier = pltpu.get_barrier_semaphore()
    partners = [(west, lat), (east, lat), (lon, above), (lon, below), (west, above), (east, below)]
    partners += [(lon, lat // 2 * 2 + 1 - core)]
    partners += [plane_id((me + s) % PEERS, xh, lat) for s in range(1, PEERS)]
    partners += [column_id((xi + s) % 4, me, core) for s in range(1, 4)]
    for device in partners:
        pl.semaphore_signal(barrier, inc=1, device_id=device, device_id_type=MESH_ID)
    pl.semaphore_wait(barrier, len(partners))

    halos = []
    for k, source in enumerate((field_ref, cot_ref)):
        first, last = source.at[:, :, pl.ds(0, HALF)], source.at[:, :, pl.ds(HALF, HALF)]
        own = pltpu.make_async_copy(last, halo_ref.at[4 * k], local_sems.at[k])
        copies = [own]
        for s, (piece, device) in enumerate(((first, (west, lat)), (last, (lon, above)), (first, (west, above)))):
            copies.append(remote(piece, halo_ref.at[4 * k + 1 + s], halo_send, halo_recv, 3 * k + s, device))
        for copy in copies:
            copy.start()
        halos.append(copies)

    def trail(value, k, own, got):
        for c in range(WC):
            rows = value[c * 64:(c + 1) * 64].astype(F32).reshape(8, 8, C)[:, 0:6, :].astype(BF)
            send_ref[2 * k + c // 6, :, :, c % 6 * C:(c % 6 + 1) * C] = rows
        first, last = send_ref.at[2 * k], send_ref.at[2 * k + 1]
        copies = [pltpu.make_async_copy(first, own, local_sems.at[2 + k])]
        for s, (piece, device) in enumerate(((last, (east, lat)), (first, (lon, below)), (last, (east, below)))):
            copies.append(remote(piece, got.at[s], trail_send, trail_recv, 3 * k + s, device))
        for copy in copies:
            copy.start()
        return copies

    sums = []
    for k, (grads, got, halves, final, terms, part, cross) in enumerate((
        (grads0, got0, halves0, final0, terms0, part0, cross0), (grads1, got1, halves1, final1, terms1, part1, cross1)
    )):
        sums.append(CoreSum(
            grads, got, halves, final, (core_send.at[k], core_recv.at[k]), ROWS[k], terms, part, cross,
            (plane_send.at[k], plane_recv.at[k]), (x_send.at[k], x_recv.at[k]), (back_send.at[k], back_recv.at[k]), local_sems.at[4 + k],
        ))
    sum0, sum1 = sums
    sum_t = PlaneSum(
        lambda p: grads_t.at[p], terms_t, part_t, cross_t, lambda p: final_t.at[p],
        (plane_send.at[2], plane_recv.at[2]), (x_send.at[2], x_recv.at[2]), (back_send.at[2], back_recv.at[2]), local_sems.at[6], True,
    )

    t_ref[...] = jnp.zeros_like(t_ref)
    for w in range(NW):
        for h in range(HEADS):
            t_ref[h * RELP:h * RELP + REL, :] = table[w, 0, h]
        left = t_ref[...]
        spread = None
        for part in range(3):
            low = left.astype(BF)
            left = left - low.astype(F32)
            moved = nn(low, pair[...]).astype(BF)
            term = tn(moved, rep[...])
            spread = term if spread is None else spread + term
        z = spread[0:16] * entry[0:1]
        for a in range(1, A):
            z = z + spread[16 * a:16 * a + 16] * entry[a:a + 1]
        hide = jnp.where(lat == lat_n - 1, differs[1], 0.0)
        if w == NW - 1:
            hide = hide + differs[0]
        z = jnp.where(hide > 0.5, MASKED, z)
        for cs in range(WC):
            bias_ref[w, cs * A:(cs + 1) * A, :] = z[0:A, (11 - cs) * HEADS * A:(11 - cs) * HEADS * A + HT]

    x_ref[...] = jnp.zeros_like(x_ref)
    for copy in halos[0]:
        copy.wait()
    gather_tokens(x_ref, halo_ref.at[0], halo_ref.at[1], halo_ref.at[2], halo_ref.at[3])
    field = tn(x_ref[...].reshape(WC * 64, C).astype(BF), perm[...])

    gain1 = column_of(gain_attn[...])
    gain2 = column_of(gain_mlp[...])
    hat1, inv1 = normalise(field)
    normed1 = (hat1 * gain1).astype(BF)
    projected = tn(qkv_w[...], normed1)
    scaling = HEAD ** (-0.5)
    q_ref[...] = (projected[0:C] * scaling).astype(BF)
    k_ref[...] = projected[C:2 * C].astype(BF)
    v_ref[...] = projected[2 * C:].astype(BF)
    kv_ref[...] = tn(normed1, qkv_w[:, C:]).astype(BF)
    mask = head_mask[...].astype(F32)

    for w in range(NW):
        rows = slice(w * TW, (w + 1) * TW)
        qblk = (nn(q_ref[:, rows], expand[...]) * mask).astype(BF)
        qblk_ref[w] = qblk
        scores = nn(kv_ref[rows, 0:C], qblk) + bias_ref[w]
        raised = jnp.exp(scores - jnp.max(scores, axis=0, keepdims=True))
        probs = raised * (1.0 / jnp.sum(raised, axis=0, keepdims=True))
        p_ref[w] = probs
        context = (nn(v_ref[:, rows], probs.astype(BF)) * mask).astype(BF)
        ctx_ref[:, rows] = nt(context, expand[...]).astype(BF)
    attended = tn(proj_w[...], ctx_ref[...]).astype(BF)

    for copy in halos[1]:
        copy.wait()
    gather_tokens(x_ref, halo_ref.at[4], halo_ref.at[5], halo_ref.at[6], halo_ref.at[7])
    cot = tn(x_ref[...].reshape(WC * 64, C).astype(BF), perm[...])
    cot_low = cot.astype(BF)

    resid = field + attended.astype(F32)
    hat2, inv2 = normalise(resid)
    normed2 = (hat2 * gain2).astype(BF)
    hidden = tn(fc1_w[...], normed2)
    k0 = 0.7978845608028654
    k1 = 0.044715
    sq = hidden * hidden
    th = jnp.tanh(hidden * (k0 + (k0 * k1) * sq))
    half = 0.5 * (1.0 + th)
    act = (hidden * half).astype(BF)
    slope = half + 0.5 * hidden * (1.0 - th * th) * (k0 + (3.0 * k0 * k1) * sq)
    d_act = nn(fc2_w[...], cot_low).astype(BF)
    d_pre = (d_act.astype(F32) * slope).astype(BF)
    fc1_grad = nt(normed2, d_pre).astype(BF)
    fc2_grad = nt(cot_low, act).astype(BF)
    for k in range(6):
        put_tiles(grads0, ROWS[0], k * C, fc1_grad[:, k * LANES:(k + 1) * LANES])
        put_tiles(grads0, ROWS[0], (6 + k) * C, fc2_grad[:, k * LANES:(k + 1) * LANES])
    d_normed2 = nn(fc1_w[...], d_pre)
    gain2_grad = row_of(jnp.sum(d_normed2 * hat2, axis=1, keepdims=True))
    d_resid = cot + normalise_back(d_normed2 * gain2, hat2, inv2)
    d_att = d_resid.astype(BF)
    proj_grad = nt(ctx_ref[...], d_att).astype(BF)
    put_tiles(grads0, ROWS[0], 12 * C, proj_grad[:, C - LANES:])
    gain_rows = jnp.concatenate([gain2_grad[:, 0:LANES], gain2_grad[:, C - LANES:], jnp.zeros((62, LANES), F32)], axis=0)
    put_tiles(grads0, ROWS[0], 13 * C, gain_rows.astype(BF))
    sum0.start_core()
    mixed = (resid + tn(fc2_w[...], act)).astype(BF)
    mixed_copies = trail(nt(perm[...], mixed).astype(BF), 0, mixed_own, mixed_got)
    dctx_ref[...] = nn(proj_w[...], d_att).astype(BF)

    for w in range(NW):
        if w == 1:
            sum0.start()
        if w == 3:
            sum0.across()
        rows = slice(w * TW, (w + 1) * TW)
        dblk = (nn(dctx_ref[:, rows], expand[...]) * mask).astype(BF)
        probs = p_ref[w]
        d_probs = nn(kv_ref[rows, C:], dblk)
        weighted = probs * d_probs
        d_scores = weighted - probs * jnp.sum(weighted, axis=0, keepdims=True)
        d_low = d_scores.astype(BF)
        dproj_ref[2 * C:, rows] = nt(dblk, probs.astype(BF)).astype(BF)
        dproj_ref[C:2 * C, rows] = nt(qblk_ref[w], d_low).astype(BF)
        d_q = (nn(k_ref[:, rows], d_low) * (mask * scaling)).astype(BF)
        dproj_ref[0:C, rows] = nt(d_q, expand[...]).astype(BF)
        z_ref[...] = jnp.zeros_like(z_ref)
        for cs in range(WC):
            at = slice((11 - cs) * HEADS * A, (11 - cs) * HEADS * A + HT)
            z_ref[0:A, at] += d_scores[cs * A:(cs + 1) * A]
        dz = z_ref[...]
        spread = jnp.concatenate([dz * entry[a:a + 1] for a in range(A)], axis=0).astype(BF)
        d_table = nt(nt(rep[...], spread).astype(BF), pair[...]).astype(BF)
        for k in range(3):
            grads_t[3 * w + k] = d_table[TROWS * k:TROWS * (k + 1), 0:LANES]
            grads_t[12 + k, :, 16 * w:16 * w + 16] = d_table[TROWS * k:TROWS * (k + 1), LANES:]
    zeros_t = jnp.zeros((TROWS, 64), BF)
    for k in range(3):
        grads_t[12 + k, :, 64:] = zeros_t
    grads_t[15] = jnp.zeros((TROWS, LANES), BF)
    sum_t.start()
    sum0.back()

    dproj = dproj_ref[...]
    qkv_grad = nt(normed1, dproj).astype(BF)
    d_win = nn(qkv_w[...], dproj).astype(BF).astype(F32)
    gain1_grad = row_of(jnp.sum(d_win * hat1, axis=1, keepdims=True))
    for k in range(4):
        put_tiles(grads1, ROWS[1], k * C, qkv_grad[:, k * LANES:(k + 1) * LANES])
    put_tiles(grads1, ROWS[1], 4 * C, jnp.concatenate([qkv_grad[:, 4 * LANES:], proj_grad[:, 0:64]], axis=1))
    gain_rows = jnp.concatenate([gain1_grad[:, 0:LANES], gain1_grad[:, C - LANES:], jnp.zeros((62, LANES), F32)], axis=0)
    put_tiles(grads1, ROWS[1], 5 * C, gain_rows.astype(BF))
    sum1.start_core()
    d_field = (d_resid + normalise_back(d_win * gain1, hat1, inv1)).astype(BF)
    fgrad_copies = trail(nt(perm[...], d_field).astype(BF), 1, fgrad_own, fgrad_got)
    sum1.start()
    sum_t.across()
    sum0.finish()
    sum1.across()
    sum_t.back()
    sum0.finish_core()
    sum1.back()
    sum_t.finish()
    sum1.finish()
    sum1.finish_core()
    for copy in mixed_copies + fgrad_copies:
        copy.wait()


def results_kernel(
    mixed_own, mixed_got, fgrad_own, fgrad_got, final0, final1, final_t,
    mixed, fgrad, qkv, proj, fc1, fc2, gain_attn, gain_mlp, table,
):
    for own, got, out in ((mixed_own, mixed_got, mixed), (fgrad_own, fgrad_got, fgrad)):
        for at, top, low in ((0, got.at[2], got.at[0]), (HALF, got.at[1], own)):
            rows = jnp.concatenate([top[...].astype(F32)[:, 3:6, :], low[...].astype(F32)[:, 0:3, :]], axis=1)
            out[:, :, at:at + HALF] = rows.astype(BF)
    for k in range(6):
        fc1[:, k * LANES:(k + 1) * LANES] = get_tiles(final0, ROWS[0], k * C, C)
        fc2[k * LANES:(k + 1) * LANES, :] = get_tiles(final0, ROWS[0], (6 + k) * C, C).T
    proj[:, 64:] = get_tiles(final0, ROWS[0], 12 * C, C)
    for k in range(4):
        qkv[:, k * LANES:(k + 1) * LANES] = get_tiles(final1, ROWS[1], k * C, C)
    shared = get_tiles(final1, ROWS[1], 4 * C, C)
    qkv[:, 4 * LANES:] = shared[:, 0:64]
    proj[:, 0:64] = shared[:, 64:]
    for out, final, row in ((gain_attn, final1, 5 * C), (gain_mlp, final0, 13 * C)):
        rows = get_tiles(final, final.shape[1], row, 16)
        out[:, 0:LANES] = rows[0:1]
        out[:, LANES:] = rows[1:2, 64:]
    for w in range(NW):
        wide = jnp.concatenate([final_t[3 * w + k].astype(F32) for k in range(3)], axis=0)
        tail = jnp.concatenate([final_t[12 + k].astype(F32) for k in range(3)], axis=0)
        for h in range(HEADS):
            table[w, 0, h, :, 0:LANES] = wide[h * RELP:h * RELP + REL]
            table[w, 0, h, :, LANES:] = tail[h * RELP:h * RELP + REL, 16 * w:16 * w + 16]


def shards(field, cotangent, gain_attn, gain_mlp, qkv_weight, proj_weight, fc1_weight, fc2_weight, bias_table):
    consts = [jnp.asarray(v) for v in constants()]
    sds = jax.ShapeDtypeStruct
    vm = pl.BlockSpec(memory_space=pltpu.VMEM)
    hbm = pl.BlockSpec(memory_space=pl.ANY)
    half = (8, 6, HALF)
    dma = pltpu.SemaphoreType.DMA
    pieces = pl.pallas_call(
        block_kernel,
        out_shape=(
            sds(half, BF), sds((3,) + half, BF), sds(half, BF), sds((3,) + half, BF),
            sds((2 * PEERS, ROWS[0], LANES), BF), sds((2 * PEERS, ROWS[1], LANES), BF), sds((PEERS, TROWS, LANES), BF),
        ),
        in_specs=[hbm] * 2 + [vm] * (7 + len(consts)),
        out_specs=(hbm,) * 7,
        scratch_shapes=[
            pltpu.VMEM((WC, 8, 8, C), F32),
            pltpu.VMEM((HEADS * RELP, TW), F32),
            pltpu.VMEM((NW, TW, HT), F32),
            pltpu.VMEM((16, ZL), F32),
            pltpu.VMEM((NW, TW, HT), F32),
            pltpu.VMEM((NW, C, HT), BF),
            pltpu.VMEM((C, TOK), BF), pltpu.VMEM((C, TOK), BF), pltpu.VMEM((C, TOK), BF),
            pltpu.VMEM((TOK, 2 * C), BF),
            pltpu.VMEM((C, TOK), BF), pltpu.VMEM((C, TOK), BF),
            pltpu.VMEM((3 * C, TOK), BF),
            pltpu.VMEM((8,) + half, BF),
            pltpu.VMEM((4,) + half, BF),
            pltpu.VMEM((2 * PEERS, ROWS[0], LANES), BF), pltpu.VMEM((2 * PEERS, ROWS[1], LANES), BF), pltpu.VMEM((PEERS, TROWS, LANES), BF),
            pltpu.VMEM((PEERS, ROWS[0], LANES), BF), pltpu.VMEM((PEERS, ROWS[1], LANES), BF),
            pltpu.VMEM((PEERS, ROWS[0], LANES), BF), pltpu.VMEM((PEERS, ROWS[1], LANES), BF),
            pltpu.VMEM((PEERS, ROWS[0], LANES), BF), pltpu.VMEM((PEERS, ROWS[1], LANES), BF), pltpu.VMEM((PEERS, TROWS, LANES), BF),
            pltpu.VMEM((ROWS[0], LANES), BF), pltpu.VMEM((ROWS[1], LANES), BF), pltpu.VMEM((TROWS, LANES), BF),
            pltpu.VMEM((4, ROWS[0], LANES), BF), pltpu.VMEM((4, ROWS[1], LANES), BF), pltpu.VMEM((2, TROWS, LANES), BF),
            dma((7,)), dma((6,)), dma((6,)), dma((6,)), dma((6,)), dma((2, 2)), dma((2, 2)),
            dma((3, PEERS)), dma((3, PEERS)), dma((3, 4)), dma((3, 4)), dma((3, PEERS)), dma((3, PEERS)),
        ],
        compiler_params=pltpu.CompilerParams(vmem_limit_bytes=56 * 1024 * 1024, collective_id=0, has_side_effects=True),
        name="block",
    )(field, cotangent, gain_attn.reshape(1, C), gain_mlp.reshape(1, C), qkv_weight, proj_weight, fc1_weight, fc2_weight, bias_table, *consts)
    tile = field.shape
    mixed, fgrad, qkv, proj, fc1, fc2, gain1, gain2, table = pl.pallas_call(
        results_kernel,
        out_shape=(
            sds(tile, BF), sds(tile, BF), sds((C, 3 * C), F32), sds((C, C), F32), sds((C, HID), F32), sds((HID, C), F32),
            sds((1, C), F32), sds((1, C), F32), sds(bias_table.shape, F32),
        ),
        in_specs=[vm] * 7,
        out_specs=(vm,) * 9,
        compiler_params=pltpu.CompilerParams(vmem_limit_bytes=32 * 1024 * 1024),
        name="results",
    )(*pieces)
    return mixed, fgrad, qkv, proj, fc1, fc2, gain1.reshape(C), gain2.reshape(C), table


def solution(mesh):
    grid = P(None, "lat", "lon")
    by_type = P(None, "lat", None, None, None)
    return jax.shard_map(
        shards,
        mesh=mesh,
        in_specs=(grid, grid) + (P(),) * 6 + (by_type,),
        out_specs=(grid, grid) + (P(),) * 6 + (by_type,),
        check_vma=False,
    )
```

```python
import functools
import jax
import jax.numpy as jnp
import numpy as np
from jax import lax
from jax.experimental import pallas as pl
from jax.experimental.pallas import tpu as pltpu
from jax.sharding import PartitionSpec as P

BF = jnp.bfloat16
F32 = jnp.float32
C = 192
HEADS = 6
HEAD = 32
HID = 768
WZ, WR, WC = 2, 6, 12
A = WZ * WR
TW = A * WC
NW = 4
TOK = NW * TW
REL = 2 * WC - 1
RELP = 24
HT = HEADS * TW
ZL = REL * HEADS * A
EPS = 1e-05
MASKED = -1000000000.0


def constants():
    perm = np.zeros((WC, WR, 8, NW, WC, WZ, WR), np.float32)
    for c in range(WC):
        for w in range(NW):
            for lev in range(WZ):
                for r in range(WR):
                    perm[c, r, (2 * w + lev + 1) % 8, w, c, lev, r] = 1
    perm = perm.reshape(TOK, TOK)
    expand = np.zeros((WC, A, WC, HEADS, A), np.float32)
    for c in range(WC):
        for a in range(A):
            expand[c, a, c, :, a] = 1
    expand = expand.reshape(TW, HT)
    head_mask = np.zeros((HEADS, HEAD, WC, HEADS, A), np.float32)
    for h in range(HEADS):
        head_mask[h, :, :, h, :] = 1
    head_mask = head_mask.reshape(C, HT)
    rep = np.zeros((HEADS, RELP, REL, HEADS, A), np.float32)
    for h in range(HEADS):
        for rel in range(REL):
            rep[h, rel, rel, h, :] = 1
    rep = rep.reshape(HEADS * RELP, ZL)
    pair = np.zeros((WZ, WZ, WR, WR, WZ, WR, 16), np.float32)
    for lt in range(WZ):
        for ls in range(WZ):
            for rt in range(WR):
                for rs in range(WR):
                    pair[lt, ls, rt, rs, lt, rt, ls * WR + rs] = 1
    pair = pair.reshape(TW, A * 16)
    lane_a = np.arange(ZL) % A
    entry = (np.arange(A)[:, None] == lane_a[None, :]).astype(np.float32)
    entry = np.concatenate([entry, np.zeros((4, ZL), np.float32)])
    b = np.arange(16)
    level_differs = ((b[:, None] // WR) != (lane_a[None, :] // WR)) & (b[:, None] < A)
    row_differs = ((b[:, None] % WR >= 3) != (lane_a[None, :] % WR >= 3)) & (b[:, None] < A)
    differs = np.stack([level_differs, row_differs]).astype(np.float32)
    return [np.asarray(v, dtype=BF) for v in (perm, expand, head_mask, rep, pair)] + [entry, differs]


def nn(a, b):
    return lax.dot_general(a, b, (((1,), (0,)), ((), ())), preferred_element_type=F32)


def nt(a, b):
    return lax.dot_general(a, b, (((1,), (1,)), ((), ())), preferred_element_type=F32)


def tn(a, b):
    return lax.dot_general(a, b, (((0,), (0,)), ((), ())), preferred_element_type=F32)


def column_of(row):
    size = row.shape[1]
    eye = lax.broadcasted_iota(jnp.int32, (size, size), 0) == lax.broadcasted_iota(jnp.int32, (size, size), 1)
    return jnp.sum(jnp.where(eye, row, 0.0), axis=1, keepdims=True)


def row_of(column):
    size = column.shape[0]
    eye = lax.broadcasted_iota(jnp.int32, (size, size), 0) == lax.broadcasted_iota(jnp.int32, (size, size), 1)
    return jnp.sum(jnp.where(eye, column, 0.0), axis=0, keepdims=True)


def normalise(v):
    centre = v - jnp.sum(v, axis=0, keepdims=True) * (1.0 / C)
    inv = lax.rsqrt(jnp.sum(centre * centre, axis=0, keepdims=True) * (1.0 / C) + EPS)
    return centre * inv, inv


def normalise_back(g, hat, inv):
    return inv * (g - jnp.sum(g, axis=0, keepdims=True) * (1.0 / C) - hat * (jnp.sum(g * hat, axis=0, keepdims=True) * (1.0 / C)))


def tokens_of(x_ref, win):
    for c in range(WC):
        x_ref[c * 48:(c + 1) * 48, :] = win[:, :, c * C:(c + 1) * C].astype(F32).reshape(48, C)
    return x_ref[...].astype(BF)


HALF = WC * C // 2
LANES = 128
PEERS = 16
ROWS = (80, 32)
TROWS = 48
MESH_ID = pl.DeviceIdType.MESH


def place():
    lon, lat = lax.axis_index("lon"), lax.axis_index("lat")
    return (lon // 4) % 2 * 2 + lat // 2, lon // 8, lon % 4, lat % 2


def device_at(x, y, z, core):
    return ((y * 2 + x // 2) * 4 + z, x % 2 * 2 + core)


def remote(src, dst, sends, recvs, k, device):
    return pltpu.make_async_remote_copy(
        src_ref=src, dst_ref=dst, send_sem=sends.at[k], recv_sem=recvs.at[k], device_id=device, device_id_type=MESH_ID
    )


def total(ref, count):
    value = ref[0].astype(F32)
    for k in range(1, count):
        value = value + ref[k].astype(F32)
    return value.astype(BF)


class PlaneSum:
    def __init__(self, axes, piece, terms, part, cross, final, plane_sems, x_sems, back_sems, local_sem):
        self.axes, self.piece, self.terms, self.part, self.cross, self.final = axes, piece, terms, part, cross, final
        self.plane_sems, self.x_sems, self.back_sems, self.local_sem = plane_sems, x_sems, back_sems, local_sem
        self.at = place()
        self.me = self.at[axes[0]] * 4 + self.at[axes[1]]
        self.count = cross.shape[0]
        self.step = 4 // self.count
        self.mine = self.at[axes[2]] // self.step

    def in_plane(self, s):
        p = (self.me + s) % PEERS
        at = list(self.at)
        at[self.axes[0]], at[self.axes[1]] = p // 4, p % 4
        return p, device_at(*at)

    def along(self, s):
        at = list(self.at)
        at[self.axes[2]] = (at[self.axes[2]] + s * self.step) % 4
        return device_at(*at)

    def partners(self):
        return [self.in_plane(s)[1] for s in range(1, PEERS)] + [self.along(s) for s in range(1, self.count)]

    def start(self):
        self.copies = []
        for s in range(1, PEERS):
            p, device = self.in_plane(s)
            copy = remote(self.piece(p), self.terms.at[s], *self.plane_sems, s, device)
            copy.start()
            self.copies.append(copy)

    def across(self):
        self.terms[0] = self.piece(self.me)[...]
        for copy in self.copies:
            copy.wait()
        value = total(self.terms, PEERS)
        self.part[...] = value
        self.cross[self.mine] = value
        self.copies = []
        for s in range(1, self.count):
            copy = remote(self.part, self.cross.at[self.mine], *self.x_sems, s, self.along(s))
            copy.start()
            self.copies.append(copy)

    def back(self):
        for copy in self.copies:
            copy.wait()
        self.part[...] = total(self.cross, self.count)
        self.own = pltpu.make_async_copy(self.part, self.final(self.me), self.local_sem)
        self.own.start()
        self.copies = []
        for s in range(1, PEERS):
            copy = remote(self.part, self.final(self.me), *self.back_sems, s, self.in_plane(s)[1])
            copy.start()
            self.copies.append(copy)

    def finish(self):
        self.own.wait()
        for copy in self.copies:
            copy.wait()


class CoreSum(PlaneSum):
    def __init__(self, axes, grads, got, halves, final, core_sems, terms, part, cross, *sems):
        self.grads, self.got, self.halves, self.whole, self.core_sems = grads, got, halves, final, core_sems
        core = place()[3]
        super().__init__(axes, lambda p: halves.at[p], terms, part, cross, lambda p: final.at[core * PEERS + p], *sems)
        self.core = core
        self.other = device_at(*self.at[:3], 1 - core)

    def partners(self):
        return [self.other] + super().partners()

    def start_core(self):
        self.swap = remote(self.grads.at[pl.ds((1 - self.core) * PEERS, PEERS)], self.got, *self.core_sems, 0, self.other)
        self.swap.start()

    def start(self):
        self.swap.wait()
        for p in range(PEERS):
            self.halves[p] = (self.grads[self.core * PEERS + p].astype(F32) + self.got[p].astype(F32)).astype(BF)
        super().start()

    def finish(self):
        super().finish()
        mine = self.whole.at[pl.ds(self.core * PEERS, PEERS)]
        self.swap = remote(mine, mine, *self.core_sems, 1, self.other)
        self.swap.start()

    def finish_core(self):
        self.swap.wait()


def put_tiles(ref, rows, first, value):
    done = 0
    while done < value.shape[0]:
        piece, row = divmod(first + done, rows)
        count = min(rows - row, value.shape[0] - done)
        ref[piece, row:row + count, :] = value[done:done + count]
        done += count


def get_tiles(ref, rows, first, count):
    parts, done = [], 0
    while done < count:
        piece, row = divmod(first + done, rows)
        take = min(rows - row, count - done)
        parts.append(ref[piece, row:row + take, :].astype(F32))
        done += take
    return parts[0] if len(parts) == 1 else jnp.concatenate(parts, axis=0)


def block_kernel(
    field_ref, cot_ref, *refs,
):
    count = 14
    sources, outs, (held, rest) = refs[:count], refs[count:count + 5], (refs[count + 5:2 * count + 5], refs[2 * count + 5:])
    block(field_ref, cot_ref, sources, held, *outs, *rest)


def block(
    field_ref, cot_ref, sources, held,
    mixed_out, fgrad_out, final0, final1, final_t,
    x_ref, t_ref, bias_ref, z_ref, p_ref, qblk_ref, q_ref, k_ref, v_ref, kv_ref, ctx_ref, dctx_ref, dproj_ref,
    win_ref, send_ref, grads0, grads1, grads_t, got0, got1, halves0, halves1,
    terms0, terms1, terms_t, part0, part1, part_t, cross0, cross1, cross_t,
    load_sems, local_sems, halo_send, halo_recv, trail_send, trail_recv, core_send, core_recv,
    plane_send, plane_recv, x_send, x_recv, back_send, back_recv,
):
    gain_attn, gain_mlp, qkv_w, proj_w, fc1_w, fc2_w, table, perm, expand, head_mask, rep, pair, entry, differs = held
    lon, lat = lax.axis_index("lon"), lax.axis_index("lat")
    lon_n, lat_n = 32, 4
    west, east = (lon + lon_n - 1) % lon_n, (lon + 1) % lon_n
    above, below = (lat + lat_n - 1) % lat_n, (lat + 1) % lat_n

    sum0, sum1 = [
        CoreSum(
            axes, grads, got, halves, final, (core_send.at[k], core_recv.at[k]), terms, part, cross,
            (plane_send.at[k], plane_recv.at[k]), (x_send.at[k], x_recv.at[k]), (back_send.at[k], back_recv.at[k]), local_sems.at[4 + k],
        )
        for k, (axes, grads, got, halves, final, terms, part, cross) in enumerate((
            ((0, 1, 2), grads0, got0, halves0, final0, terms0, part0, cross0),
            ((0, 2, 1), grads1, got1, halves1, final1, terms1, part1, cross1),
        ))
    ]
    sum_t = PlaneSum(
        (1, 2, 0), lambda p: grads_t.at[p], terms_t, part_t, cross_t, lambda p: final_t.at[p],
        (plane_send.at[2], plane_recv.at[2]), (x_send.at[2], x_recv.at[2]), (back_send.at[2], back_recv.at[2]), local_sems.at[6],
    )

    barrier = pltpu.get_barrier_semaphore()
    partners = [(west, lat), (east, lat), (lon, above), (lon, below), (west, above), (east, below)]
    partners += sum_t.partners() + sum0.partners() + sum1.partners()
    for device in partners:
        pl.semaphore_signal(barrier, inc=1, device_id=device, device_id_type=MESH_ID)
    loads = [pltpu.make_async_copy(a, b, load_sems.at[k]) for k, (a, b) in enumerate(zip(sources, held))]
    first = (6, 11, 10, 12, 13)
    for k in first + tuple(k for k in range(len(loads)) if k not in first):
        loads[k].start()
    pl.semaphore_wait(barrier, len(partners))

    right, left = pl.ds(HALF, HALF), pl.ds(0, HALF)
    upper, lower = pl.ds(0, 3), pl.ds(3, 3)
    halos = []
    for k, source in enumerate((field_ref, cot_ref)):
        win = win_ref.at[k]
        copies = [pltpu.make_async_copy(source.at[lower, :, right], win.at[upper, :, left], local_sems.at[k])]
        for s, (rows, cols, device) in enumerate((((lower, upper), (left, right), (west, lat)), ((upper, lower), (right, left), (lon, above)), ((upper, lower), (left, right), (west, above)))):
            copies.append(remote(source.at[rows[0], :, cols[0]], win.at[rows[1], :, cols[1]], halo_send, halo_recv, 3 * k + s, device))
        halos.append(copies)
    for copy in halos[0]:
        copy.start()

    def trail(value, k, out):
        win = send_ref.at[k]
        back = nt(perm[...], value)
        for c in range(WC):
            win[:, :, c * C:(c + 1) * C] = back[c * 48:(c + 1) * 48].reshape(WR, 8, C).astype(BF)
        copies = [pltpu.make_async_copy(win.at[upper, :, left], out.at[lower, :, right], local_sems.at[2 + k])]
        for s, (rows, cols, device) in enumerate((((upper, lower), (right, left), (east, lat)), ((lower, upper), (left, right), (lon, below)), ((lower, upper), (right, left), (east, below)))):
            copies.append(remote(win.at[rows[0], :, cols[0]], out.at[rows[1], :, cols[1]], trail_send, trail_recv, 3 * k + s, device))
        for copy in copies:
            copy.start()
        return copies

    for k in first:
        loads[k].wait()
    t_ref[...] = jnp.zeros_like(t_ref)
    for w in range(NW):
        for h in range(HEADS):
            t_ref[h * RELP:h * RELP + REL, :] = table[w, h, :, 0, :]
        rest = t_ref[...]
        spread = None
        for part in range(3):
            low = rest.astype(BF)
            rest = rest - low.astype(F32)
            moved = nn(low, pair[...]).astype(BF)
            term = tn(moved, rep[...])
            spread = term if spread is None else spread + term
        z = spread[0:16] * entry[0:1]
        for a in range(1, A):
            z = z + spread[16 * a:16 * a + 16] * entry[a:a + 1]
        hide = jnp.where(lat == lat_n - 1, differs[1], 0.0)
        if w == NW - 1:
            hide = hide + differs[0]
        z = jnp.where(hide > 0.5, MASKED, z)
        for cs in range(WC):
            bias_ref[w, cs * A:(cs + 1) * A, :] = z[0:A, (11 - cs) * HEADS * A:(11 - cs) * HEADS * A + HT]

    for k in range(len(loads)):
        if k not in first:
            loads[k].wait()
    for copy in halos[0]:
        copy.wait()
    for copy in halos[1]:
        copy.start()
    field = tn(tokens_of(x_ref, win_ref.at[0]), perm[...])

    gain1 = column_of(gain_attn[...])
    gain2 = column_of(gain_mlp[...])
    hat1, inv1 = normalise(field)
    normed1 = (hat1 * gain1).astype(BF)
    projected = tn(qkv_w[...], normed1)
    scaling = HEAD ** (-0.5)
    q_ref[...] = (projected[0:C] * scaling).astype(BF)
    k_ref[...] = projected[C:2 * C].astype(BF)
    v_ref[...] = projected[2 * C:].astype(BF)
    kv_ref[...] = tn(normed1, qkv_w[:, C:]).astype(BF)
    mask = head_mask[...].astype(F32)

    for w in range(NW):
        rows = slice(w * TW, (w + 1) * TW)
        qblk = (nn(q_ref[:, rows], expand[...]) * mask).astype(BF)
        qblk_ref[w] = qblk
        scores = nn(kv_ref[rows, 0:C], qblk) + bias_ref[w]
        raised = jnp.exp(scores - jnp.max(scores, axis=0, keepdims=True))
        probs = raised * (1.0 / jnp.sum(raised, axis=0, keepdims=True))
        p_ref[w] = probs
        context = (nn(v_ref[:, rows], probs.astype(BF)) * mask).astype(BF)
        ctx_ref[:, rows] = nt(context, expand[...]).astype(BF)
    attended = tn(proj_w[...], ctx_ref[...]).astype(BF)

    for copy in halos[1]:
        copy.wait()
    cot = tn(tokens_of(x_ref, win_ref.at[1]), perm[...])
    cot_low = cot.astype(BF)

    resid = field + attended.astype(F32)
    hat2, inv2 = normalise(resid)
    normed2 = (hat2 * gain2).astype(BF)
    hidden = tn(fc1_w[...], normed2)
    k0 = 0.7978845608028654
    k1 = 0.044715
    sq = hidden * hidden
    th = jnp.tanh(hidden * (k0 + (k0 * k1) * sq))
    half = 0.5 * (1.0 + th)
    act = (hidden * half).astype(BF)
    slope = half + 0.5 * hidden * (1.0 - th * th) * (k0 + (3.0 * k0 * k1) * sq)
    d_act = tn(fc2_w[...], cot_low).astype(BF)
    d_pre = (d_act.astype(F32) * slope).astype(BF)
    fc1_grad = nt(normed2, d_pre).astype(BF)
    fc2_grad = nt(cot_low, act).astype(BF)
    for k in range(6):
        put_tiles(grads0, ROWS[0], k * C, fc1_grad[:, k * LANES:(k + 1) * LANES])
        put_tiles(grads0, ROWS[0], (6 + k) * C, fc2_grad[:, k * LANES:(k + 1) * LANES])
    d_normed2 = nn(fc1_w[...], d_pre)
    gain2_grad = row_of(jnp.sum(d_normed2 * hat2, axis=1, keepdims=True))
    d_resid = cot + normalise_back(d_normed2 * gain2, hat2, inv2)
    d_att = d_resid.astype(BF)
    proj_grad = nt(ctx_ref[...], d_att).astype(BF)
    put_tiles(grads0, ROWS[0], 12 * C, proj_grad[:, C - LANES:])
    gain_rows = jnp.concatenate([gain2_grad[:, 0:LANES], gain2_grad[:, C - LANES:], jnp.zeros((62, LANES), F32)], axis=0)
    put_tiles(grads0, ROWS[0], 13 * C, gain_rows.astype(BF))
    sum0.start_core()
    dctx_ref[...] = nn(proj_w[...], d_att).astype(BF)

    for w in range(NW):
        if w == 2:
            sum0.start()
        rows = slice(w * TW, (w + 1) * TW)
        dblk = (nn(dctx_ref[:, rows], expand[...]) * mask).astype(BF)
        probs = p_ref[w]
        d_probs = nn(kv_ref[rows, C:], dblk)
        weighted = probs * d_probs
        d_scores = weighted - probs * jnp.sum(weighted, axis=0, keepdims=True)
        d_low = d_scores.astype(BF)
        dproj_ref[2 * C:, rows] = nt(dblk, probs.astype(BF)).astype(BF)
        dproj_ref[C:2 * C, rows] = nt(qblk_ref[w], d_low).astype(BF)
        d_q = (nn(k_ref[:, rows], d_low) * (mask * scaling)).astype(BF)
        dproj_ref[0:C, rows] = nt(d_q, expand[...]).astype(BF)
        p_ref[w] = d_scores

    dproj = dproj_ref[...]
    qkv_grad = nt(normed1, dproj).astype(BF)
    d_win = nn(qkv_w[...], dproj).astype(BF).astype(F32)
    gain1_grad = row_of(jnp.sum(d_win * hat1, axis=1, keepdims=True))
    for k in range(4):
        put_tiles(grads1, ROWS[1], k * C, qkv_grad[:, k * LANES:(k + 1) * LANES])
    put_tiles(grads1, ROWS[1], 4 * C, jnp.concatenate([qkv_grad[:, 4 * LANES:], proj_grad[:, 0:64]], axis=1))
    gain_rows = jnp.concatenate([gain1_grad[:, 0:LANES], gain1_grad[:, C - LANES:], jnp.zeros((62, LANES), F32)], axis=0)
    put_tiles(grads1, ROWS[1], 5 * C, gain_rows.astype(BF))
    sum1.start_core()

    for w in range(NW):
        z_ref[...] = jnp.zeros_like(z_ref)
        for cs in range(WC):
            at = slice((11 - cs) * HEADS * A, (11 - cs) * HEADS * A + HT)
            z_ref[0:A, at] += p_ref[w, cs * A:(cs + 1) * A, :]
        dz = z_ref[...]
        spread = jnp.concatenate([dz * entry[a:a + 1] for a in range(A)], axis=0).astype(BF)
        d_table = nt(nt(rep[...], spread).astype(BF), pair[...]).astype(BF)
        for k in range(3):
            grads_t[3 * w + k] = d_table[TROWS * k:TROWS * (k + 1), 0:LANES]
            grads_t[12 + k, :, 16 * w:16 * w + 16] = d_table[TROWS * k:TROWS * (k + 1), LANES:]
        if w == 1:
            sum1.start()
    for k in range(3):
        grads_t[12 + k, :, 64:] = jnp.zeros((TROWS, 64), BF)
    grads_t[15] = jnp.zeros((TROWS, LANES), BF)
    sum_t.start()

    d_field = (d_resid + normalise_back(d_win * gain1, hat1, inv1)).astype(BF)
    fgrad_copies = trail(d_field, 1, fgrad_out)
    sum0.across()
    mixed = (resid + nn(fc2_w[...], act)).astype(BF)
    mixed_copies = trail(mixed, 0, mixed_out)
    sum1.across()
    sum0.back()
    sum_t.across()
    sum1.back()
    sum_t.back()
    sum0.finish()
    sum1.finish()
    sum_t.finish()
    sum0.finish_core()
    sum1.finish_core()
    for copy in mixed_copies + fgrad_copies:
        copy.wait()


def results_kernel(
    mixed_in, fgrad_in, final0_in, final1_in, final_t_in,
    mixed, fgrad, qkv, proj, fc1, fc2, gain_attn, gain_mlp, table,
    final0, final1, final_t, through, sems,
):
    copies = [pltpu.make_async_copy(a, b, sems.at[k]) for k, (a, b) in enumerate((
        (mixed_in, through.at[0]), (fgrad_in, through.at[1]), (final0_in, final0), (final1_in, final1), (final_t_in, final_t),
    ))]
    for copy in copies:
        copy.start()
    outward = []
    for k, out in enumerate((mixed, fgrad)):
        copies[k].wait()
        outward.append(pltpu.make_async_copy(through.at[k], out, sems.at[5 + k]))
        outward[k].start()
    for copy in copies[2:]:
        copy.wait()
    for k in range(6):
        fc1[:, k * LANES:(k + 1) * LANES] = get_tiles(final0, ROWS[0], k * C, C)
        fc2[:, k * LANES:(k + 1) * LANES] = get_tiles(final0, ROWS[0], (6 + k) * C, C)
    proj[:, 64:] = get_tiles(final0, ROWS[0], 12 * C, C)
    for k in range(4):
        qkv[:, k * LANES:(k + 1) * LANES] = get_tiles(final1, ROWS[1], k * C, C)
    shared = get_tiles(final1, ROWS[1], 4 * C, C)
    qkv[:, 4 * LANES:] = shared[:, 0:64]
    proj[:, 0:64] = shared[:, 64:]
    for out, final, row in ((gain_attn, final1, 5 * C), (gain_mlp, final0, 13 * C)):
        rows = get_tiles(final, final.shape[1], row, 16)
        out[:, 0:LANES] = rows[0:1]
        out[:, LANES:] = rows[1:2, 64:]
    for w in range(NW):
        wide = jnp.concatenate([final_t[3 * w + k].astype(F32) for k in range(3)], axis=0)
        tail = jnp.concatenate([final_t[12 + k].astype(F32) for k in range(3)], axis=0)
        for h in range(HEADS):
            table[w, h, :, 0, 0:LANES] = wide[h * RELP:h * RELP + REL]
            table[w, h, :, 0, LANES:] = tail[h * RELP:h * RELP + REL, 16 * w:16 * w + 16]
    for copy in outward:
        copy.wait()


def shards(field, cotangent, gain_attn, gain_mlp, qkv_weight, proj_weight, fc1_weight, fc2_weight, bias_table):
    consts = [jnp.asarray(v) for v in constants()]
    sds = jax.ShapeDtypeStruct
    vm = pl.BlockSpec(memory_space=pltpu.VMEM)
    hbm = pl.BlockSpec(memory_space=pl.ANY)
    levels, rows, flat = field.shape
    tile = (rows, levels, flat)
    dma = pltpu.SemaphoreType.DMA
    operands = [
        field.transpose(1, 0, 2), cotangent.transpose(1, 0, 2), gain_attn.reshape(1, C), gain_mlp.reshape(1, C),
        qkv_weight, proj_weight, fc1_weight, fc2_weight.T, bias_table.transpose(0, 2, 3, 1, 4), *consts,
    ]
    pieces = pl.pallas_call(
        block_kernel,
        out_shape=(
            sds(tile, BF), sds(tile, BF),
            sds((2 * PEERS, ROWS[0], LANES), BF), sds((2 * PEERS, ROWS[1], LANES), BF), sds((PEERS, TROWS, LANES), BF),
        ),
        in_specs=[hbm] * len(operands),
        out_specs=(hbm,) * 5,
        scratch_shapes=[pltpu.VMEM(v.shape, v.dtype) for v in operands[2:]] + [
            pltpu.VMEM((TOK, C), F32),
            pltpu.VMEM((HEADS * RELP, TW), F32),
            pltpu.VMEM((NW, TW, HT), F32),
            pltpu.VMEM((16, ZL), F32),
            pltpu.VMEM((NW, TW, HT), F32),
            pltpu.VMEM((NW, C, HT), BF),
            pltpu.VMEM((C, TOK), BF), pltpu.VMEM((C, TOK), BF), pltpu.VMEM((C, TOK), BF),
            pltpu.VMEM((TOK, 2 * C), BF),
            pltpu.VMEM((C, TOK), BF), pltpu.VMEM((C, TOK), BF),
            pltpu.VMEM((3 * C, TOK), BF),
            pltpu.VMEM((2,) + tile, BF),
            pltpu.VMEM((2,) + tile, BF),
            pltpu.VMEM((2 * PEERS, ROWS[0], LANES), BF), pltpu.VMEM((2 * PEERS, ROWS[1], LANES), BF), pltpu.VMEM((PEERS, TROWS, LANES), BF),
            pltpu.VMEM((PEERS, ROWS[0], LANES), BF), pltpu.VMEM((PEERS, ROWS[1], LANES), BF),
            pltpu.VMEM((PEERS, ROWS[0], LANES), BF), pltpu.VMEM((PEERS, ROWS[1], LANES), BF),
            pltpu.VMEM((PEERS, ROWS[0], LANES), BF), pltpu.VMEM((PEERS, ROWS[1], LANES), BF), pltpu.VMEM((PEERS, TROWS, LANES), BF),
            pltpu.VMEM((ROWS[0], LANES), BF), pltpu.VMEM((ROWS[1], LANES), BF), pltpu.VMEM((TROWS, LANES), BF),
            pltpu.VMEM((4, ROWS[0], LANES), BF), pltpu.VMEM((4, ROWS[1], LANES), BF), pltpu.VMEM((2, TROWS, LANES), BF),
            dma((len(operands) - 2,)), dma((7,)), dma((6,)), dma((6,)), dma((6,)), dma((6,)), dma((2, 2)), dma((2, 2)),
            dma((3, PEERS)), dma((3, PEERS)), dma((3, 4)), dma((3, 4)), dma((3, PEERS)), dma((3, PEERS)),
        ],
        compiler_params=pltpu.CompilerParams(vmem_limit_bytes=56 * 1024 * 1024, collective_id=0, has_side_effects=True),
        name="block",
    )(
        *operands
    )
    mixed, fgrad, qkv, proj, fc1, fc2, gain1, gain2, table = pl.pallas_call(
        results_kernel,
        out_shape=(
            sds(tile, BF), sds(tile, BF), sds((C, 3 * C), F32), sds((C, C), F32), sds((C, HID), F32), sds((C, HID), F32),
            sds((1, C), F32), sds((1, C), F32), sds((NW, HEADS, REL, 1, TW), F32),
        ),
        in_specs=[hbm] * 5,
        out_specs=(hbm,) * 2 + (vm,) * 7,
        scratch_shapes=[
            pltpu.VMEM((2 * PEERS, ROWS[0], LANES), BF), pltpu.VMEM((2 * PEERS, ROWS[1], LANES), BF), pltpu.VMEM((PEERS, TROWS, LANES), BF),
            pltpu.VMEM((2,) + tile, BF),
            dma((7,)),
        ],
        compiler_params=pltpu.CompilerParams(vmem_limit_bytes=60 * 1024 * 1024),
        name="results",
    )(*pieces)
    return (
        mixed.transpose(1, 0, 2), fgrad.transpose(1, 0, 2), qkv, proj, fc1, fc2.T,
        gain1.reshape(C), gain2.reshape(C), table.transpose(0, 3, 1, 2, 4),
    )


def solution(mesh):
    grid = P(None, "lat", "lon")
    by_type = P(None, "lat", None, None, None)
    return jax.shard_map(
        shards,
        mesh=mesh,
        in_specs=(grid, grid) + (P(),) * 6 + (by_type,),
        out_specs=(grid, grid) + (P(),) * 6 + (by_type,),
        check_vma=False,
    )
```

```python
import functools
import jax
import jax.numpy as jnp
import numpy as np
from jax import lax
from jax.experimental import pallas as pl
from jax.experimental.pallas import tpu as pltpu
from jax.sharding import PartitionSpec as P

BF = jnp.bfloat16
F32 = jnp.float32
C = 192
HEADS = 6
HEAD = 32
HID = 768
WZ, WR, WC = 2, 6, 12
A = WZ * WR
TW = A * WC
NW = 4
TOK = NW * TW
REL = 2 * WC - 1
RELP = 24
HT = HEADS * TW
ZL = REL * HEADS * A
EPS = 1e-05
MASKED = -1000000000.0


def constants():
    perm = np.zeros((WC, WR, 8, NW, WC, WZ, WR), np.float32)
    for c in range(WC):
        for w in range(NW):
            for lev in range(WZ):
                for r in range(WR):
                    perm[c, r, (2 * w + lev + 1) % 8, w, c, lev, r] = 1
    perm = perm.reshape(TOK, TOK)
    expand = np.zeros((WC, A, WC, HEADS, A), np.float32)
    for c in range(WC):
        for a in range(A):
            expand[c, a, c, :, a] = 1
    expand = expand.reshape(TW, HT)
    head_mask = np.zeros((HEADS, HEAD, WC, HEADS, A), np.float32)
    for h in range(HEADS):
        head_mask[h, :, :, h, :] = 1
    head_mask = head_mask.reshape(C, HT)
    rep = np.zeros((HEADS, RELP, REL, HEADS, A), np.float32)
    for h in range(HEADS):
        for rel in range(REL):
            rep[h, rel, rel, h, :] = 1
    rep = rep.reshape(HEADS * RELP, ZL)
    pair = np.zeros((WZ, WZ, WR, WR, WZ, WR, 16), np.float32)
    for lt in range(WZ):
        for ls in range(WZ):
            for rt in range(WR):
                for rs in range(WR):
                    pair[lt, ls, rt, rs, lt, rt, ls * WR + rs] = 1
    pair = pair.reshape(TW, A * 16)
    lane_a = np.arange(ZL) % A
    entry = (np.arange(A)[:, None] == lane_a[None, :]).astype(np.float32)
    entry = np.concatenate([entry, np.zeros((4, ZL), np.float32)])
    b = np.arange(16)
    level_differs = ((b[:, None] // WR) != (lane_a[None, :] // WR)) & (b[:, None] < A)
    row_differs = ((b[:, None] % WR >= 3) != (lane_a[None, :] % WR >= 3)) & (b[:, None] < A)
    differs = np.stack([level_differs, row_differs]).astype(np.float32)
    return [np.asarray(v, dtype=BF) for v in (perm, expand, head_mask, rep, pair)] + [entry, differs]


def nn(a, b):
    return lax.dot_general(a, b, (((1,), (0,)), ((), ())), preferred_element_type=F32)


def nt(a, b):
    return lax.dot_general(a, b, (((1,), (1,)), ((), ())), preferred_element_type=F32)


def tn(a, b):
    return lax.dot_general(a, b, (((0,), (0,)), ((), ())), preferred_element_type=F32)


def column_of(row):
    size = row.shape[1]
    eye = lax.broadcasted_iota(jnp.int32, (size, size), 0) == lax.broadcasted_iota(jnp.int32, (size, size), 1)
    return jnp.sum(jnp.where(eye, row, 0.0), axis=1, keepdims=True)


def row_of(column):
    size = column.shape[0]
    eye = lax.broadcasted_iota(jnp.int32, (size, size), 0) == lax.broadcasted_iota(jnp.int32, (size, size), 1)
    return jnp.sum(jnp.where(eye, column, 0.0), axis=0, keepdims=True)


def normalise(v):
    centre = v - jnp.sum(v, axis=0, keepdims=True) * (1.0 / C)
    inv = lax.rsqrt(jnp.sum(centre * centre, axis=0, keepdims=True) * (1.0 / C) + EPS)
    return centre * inv, inv


def normalise_back(g, hat, inv):
    return inv * (g - jnp.sum(g, axis=0, keepdims=True) * (1.0 / C) - hat * (jnp.sum(g * hat, axis=0, keepdims=True) * (1.0 / C)))


def tokens_of(x_ref, win):
    for c in range(WC):
        x_ref[c * 48:(c + 1) * 48, :] = win[:, :, c * C:(c + 1) * C].astype(F32).reshape(48, C)
    return x_ref[...].astype(BF)


HALF = WC * C // 2
LANES = 128
PEERS = 16
ROWS = (80, 32)
TROWS = 48
MESH_ID = pl.DeviceIdType.MESH


def place():
    lon, lat = lax.axis_index("lon"), lax.axis_index("lat")
    return (lon // 4) % 2 * 2 + lat // 2, lon // 8, lon % 4, lat % 2


def device_at(x, y, z, core):
    return ((y * 2 + x // 2) * 4 + z, x % 2 * 2 + core)


def remote(src, dst, send_sem, recv_sem, device):
    return pltpu.make_async_remote_copy(
        src_ref=src, dst_ref=dst, send_sem=send_sem, recv_sem=recv_sem, device_id=device, device_id_type=MESH_ID
    )


def drain(like, sem):
    pltpu.make_async_copy(like, like, sem).wait()


def total(ref, count):
    value = ref[0].astype(F32)
    for k in range(1, count):
        value = value + ref[k].astype(F32)
    return value.astype(BF)


class PlaneSum:
    def __init__(self, axes, piece, terms, part, cross, final, sends, recvs):
        self.axes, self.piece, self.terms, self.part, self.cross, self.final = axes, piece, terms, part, cross, final
        self.sends, self.recvs = sends, recvs
        self.at = place()
        self.me = self.at[axes[0]] * 4 + self.at[axes[1]]
        self.count = cross.shape[0]
        self.step = 4 // self.count
        self.mine = self.at[axes[2]] // self.step
        self.others = terms.at[pl.ds(1, PEERS - 1)]
        self.few = cross.at[pl.ds(1, self.count - 1)]

    def in_plane(self, s):
        p = (self.me + s) % PEERS
        at = list(self.at)
        at[self.axes[0]], at[self.axes[1]] = p // 4, p % 4
        return p, device_at(*at)

    def along(self, s):
        at = list(self.at)
        at[self.axes[2]] = (at[self.axes[2]] + s * self.step) % 4
        return device_at(*at)

    def start(self):
        for s in range(1, PEERS):
            p, device = self.in_plane(s)
            remote(self.piece(p), self.terms.at[s], self.sends.at[0], self.recvs.at[0], device).start()

    def across(self):
        self.terms[0] = self.piece(self.me)[...]
        drain(self.others, self.recvs.at[0])
        value = total(self.terms, PEERS)
        self.part[0] = value
        self.cross[self.mine] = value
        for s in range(1, self.count):
            remote(self.part.at[0], self.cross.at[self.mine], self.sends.at[1], self.recvs.at[1], self.along(s)).start()

    def back(self):
        drain(self.few, self.recvs.at[1])
        value = total(self.cross, self.count)
        self.part[1] = value
        self.final[self.first + self.me] = value
        for s in range(1, PEERS):
            remote(self.part.at[1], self.final.at[self.first + self.me], self.sends.at[2], self.recvs.at[2], self.in_plane(s)[1]).start()

    def finish(self):
        drain(self.others, self.recvs.at[2])

    def finish_sends(self):
        drain(self.others, self.sends.at[0])
        drain(self.few, self.sends.at[1])
        drain(self.others, self.sends.at[2])

    first = 0


class CoreSum(PlaneSum):
    def __init__(self, axes, grads, got, halves, final, core_sems, *args):
        self.grads, self.got, self.halves, self.core_sems = grads, got, halves, core_sems
        super().__init__(axes, lambda p: halves.at[p], *args[:3], final, *args[3:])
        self.core = self.at[3]
        self.first = self.core * PEERS
        self.other = device_at(*self.at[:3], 1 - self.core)

    def start_core(self):
        self.swap = remote(self.grads.at[pl.ds((1 - self.core) * PEERS, PEERS)], self.got, self.core_sems[0].at[0], self.core_sems[1].at[0], self.other)
        self.swap.start()

    def start(self):
        self.swap.wait()
        for p in range(PEERS):
            self.halves[p] = (self.grads[self.core * PEERS + p].astype(F32) + self.got[p].astype(F32)).astype(BF)
        super().start()

    def finish(self):
        super().finish()
        mine = self.final.at[pl.ds(self.first, PEERS)]
        self.swap = remote(mine, mine, self.core_sems[0].at[1], self.core_sems[1].at[1], self.other)
        self.swap.start()

    def finish_core(self):
        self.swap.wait()


def put_tiles(ref, rows, first, value):
    done = 0
    while done < value.shape[0]:
        piece, row = divmod(first + done, rows)
        count = min(rows - row, value.shape[0] - done)
        ref[piece, row:row + count, :] = value[done:done + count]
        done += count


def get_tiles(ref, rows, first, count):
    parts, done = [], 0
    while done < count:
        piece, row = divmod(first + done, rows)
        take = min(rows - row, count - done)
        parts.append(ref[piece, row:row + take, :].astype(F32))
        done += take
    return parts[0] if len(parts) == 1 else jnp.concatenate(parts, axis=0)


def block_kernel(
    field_ref, cot_ref, *refs,
):
    count = 14
    sources, outs, (held, rest) = refs[:count], refs[count:count + 5], (refs[count + 5:2 * count + 5], refs[2 * count + 5:])
    block(field_ref, cot_ref, sources, held, *outs, *rest)


def block(
    field_ref, cot_ref, sources, held,
    mixed_out, fgrad_out, final0, final1, final_t,
    x_ref, t_ref, bias_ref, z_ref, p_ref, qblk_ref, q_ref, k_ref, v_ref, kv_ref, ctx_ref, dctx_ref, dproj_ref,
    win_ref, send_ref, grads0, grads1, grads_t, got0, got1, halves0, halves1,
    terms0, terms1, terms_t, part0, part1, part_t, cross0, cross1, cross_t,
    load_sems, local_sems, halo_send, halo_recv, trail_send, trail_recv, core_send, core_recv,
    sum_send, sum_recv,
):
    gain_attn, gain_mlp, qkv_w, proj_w, fc1_w, fc2_w, table, perm, expand, head_mask, rep, pair, entry, differs = held
    lon, lat = lax.axis_index("lon"), lax.axis_index("lat")
    lon_n, lat_n = 32, 4
    west, east = (lon + lon_n - 1) % lon_n, (lon + 1) % lon_n
    above, below = (lat + lat_n - 1) % lat_n, (lat + 1) % lat_n

    sum0, sum1 = [
        CoreSum((0, 1, 2), grads, got, halves, final, (core_send.at[k], core_recv.at[k]), terms, part, cross, sum_send.at[k], sum_recv.at[k])
        for k, (grads, got, halves, final, terms, part, cross) in enumerate((
            (grads0, got0, halves0, final0, terms0, part0, cross0), (grads1, got1, halves1, final1, terms1, part1, cross1),
        ))
    ]
    sum_t = PlaneSum((1, 2, 0), lambda p: grads_t.at[p], terms_t, part_t, cross_t, final_t, sum_send.at[2], sum_recv.at[2])

    barrier = pltpu.get_barrier_semaphore()
    partners = [(west, lat), (east, lat), (lon, above), (lon, below), (west, above), (east, below)]
    partners += [sum0.other] + [sum0.in_plane(s)[1] for s in range(1, PEERS)] + [sum_t.in_plane(s)[1] for s in range(1, PEERS) if s % 4]
    for device in partners:
        pl.semaphore_signal(barrier, inc=1, device_id=device, device_id_type=MESH_ID)
    loads = [pltpu.make_async_copy(a, b, load_sems.at[k]) for k, (a, b) in enumerate(zip(sources, held))]
    first = (6, 11, 10, 12, 13)
    for k in first + tuple(k for k in range(len(loads)) if k not in first):
        loads[k].start()
    pl.semaphore_wait(barrier, len(partners))

    right, left = pl.ds(HALF, HALF), pl.ds(0, HALF)
    upper, lower = pl.ds(0, 3), pl.ds(3, 3)
    halos = []
    for k, source in enumerate((field_ref, cot_ref)):
        win = win_ref.at[k]
        copies = [pltpu.make_async_copy(source.at[lower, :, right], win.at[upper, :, left], local_sems.at[k])]
        for s, (rows, cols, device) in enumerate((((lower, upper), (left, right), (west, lat)), ((upper, lower), (right, left), (lon, above)), ((upper, lower), (left, right), (west, above)))):
            copies.append(remote(source.at[rows[0], :, cols[0]], win.at[rows[1], :, cols[1]], halo_send.at[3 * k + s], halo_recv.at[3 * k + s], device))
        halos.append(copies)
    for copy in halos[0]:
        copy.start()

    def trail(value, k, out):
        win = send_ref.at[k]
        back = nt(perm[...], value)
        for c in range(WC):
            win[:, :, c * C:(c + 1) * C] = back[c * 48:(c + 1) * 48].reshape(WR, 8, C).astype(BF)
        copies = [pltpu.make_async_copy(win.at[upper, :, left], out.at[lower, :, right], local_sems.at[2 + k])]
        for s, (rows, cols, device) in enumerate((((upper, lower), (right, left), (east, lat)), ((lower, upper), (left, right), (lon, below)), ((lower, upper), (right, left), (east, below)))):
            copies.append(remote(win.at[rows[0], :, cols[0]], out.at[rows[1], :, cols[1]], trail_send.at[3 * k + s], trail_recv.at[3 * k + s], device))
        for copy in copies:
            copy.start()
        return copies

    for k in first:
        loads[k].wait()
    t_ref[...] = jnp.zeros_like(t_ref)
    for w in range(NW):
        for h in range(HEADS):
            t_ref[h * RELP:h * RELP + REL, :] = table[w, h, :, 0, :]
        rest = t_ref[...]
        spread = None
        for part in range(3):
            low = rest.astype(BF)
            rest = rest - low.astype(F32)
            moved = nn(low, pair[...]).astype(BF)
            term = tn(moved, rep[...])
            spread = term if spread is None else spread + term
        z = spread[0:16] * entry[0:1]
        for a in range(1, A):
            z = z + spread[16 * a:16 * a + 16] * entry[a:a + 1]
        hide = jnp.where(lat == lat_n - 1, differs[1], 0.0)
        if w == NW - 1:
            hide = hide + differs[0]
        z = jnp.where(hide > 0.5, MASKED, z)
        for cs in range(WC):
            bias_ref[w, cs * A:(cs + 1) * A, :] = z[0:A, (11 - cs) * HEADS * A:(11 - cs) * HEADS * A + HT]

    for k in range(len(loads)):
        if k not in first:
            loads[k].wait()
    for copy in halos[0]:
        copy.wait()
    for copy in halos[1]:
        copy.start()
    field = tn(tokens_of(x_ref, win_ref.at[0]), perm[...])

    gain1 = column_of(gain_attn[...])
    gain2 = column_of(gain_mlp[...])
    hat1, inv1 = normalise(field)
    normed1 = (hat1 * gain1).astype(BF)
    projected = tn(qkv_w[...], normed1)
    scaling = HEAD ** (-0.5)
    q_ref[...] = (projected[0:C] * scaling).astype(BF)
    k_ref[...] = projected[C:2 * C].astype(BF)
    v_ref[...] = projected[2 * C:].astype(BF)
    kv_ref[...] = tn(normed1, qkv_w[:, C:]).astype(BF)
    mask = head_mask[...].astype(F32)

    for w in range(NW):
        rows = slice(w * TW, (w + 1) * TW)
        qblk = (nn(q_ref[:, rows], expand[...]) * mask).astype(BF)
        qblk_ref[w] = qblk
        scores = nn(kv_ref[rows, 0:C], qblk) + bias_ref[w]
        raised = jnp.exp(scores - jnp.max(scores, axis=0, keepdims=True))
        probs = raised * (1.0 / jnp.sum(raised, axis=0, keepdims=True))
        p_ref[w] = probs
        context = (nn(v_ref[:, rows], probs.astype(BF)) * mask).astype(BF)
        ctx_ref[:, rows] = nt(context, expand[...]).astype(BF)
    attended = tn(proj_w[...], ctx_ref[...]).astype(BF)

    for copy in halos[1]:
        copy.wait()
    cot = tn(tokens_of(x_ref, win_ref.at[1]), perm[...])
    cot_low = cot.astype(BF)

    resid = field + attended.astype(F32)
    hat2, inv2 = normalise(resid)
    normed2 = (hat2 * gain2).astype(BF)
    hidden = tn(fc1_w[...], normed2)
    k0 = 0.7978845608028654
    k1 = 0.044715
    sq = hidden * hidden
    th = jnp.tanh(hidden * (k0 + (k0 * k1) * sq))
    half = 0.5 * (1.0 + th)
    act = (hidden * half).astype(BF)
    slope = half + 0.5 * hidden * (1.0 - th * th) * (k0 + (3.0 * k0 * k1) * sq)
    d_act = tn(fc2_w[...], cot_low).astype(BF)
    d_pre = (d_act.astype(F32) * slope).astype(BF)
    fc1_grad = nt(normed2, d_pre).astype(BF)
    fc2_grad = nt(cot_low, act).astype(BF)
    for k in range(6):
        put_tiles(grads0, ROWS[0], k * C, fc1_grad[:, k * LANES:(k + 1) * LANES])
        put_tiles(grads0, ROWS[0], (6 + k) * C, fc2_grad[:, k * LANES:(k + 1) * LANES])
    d_normed2 = nn(fc1_w[...], d_pre)
    gain2_grad = row_of(jnp.sum(d_normed2 * hat2, axis=1, keepdims=True))
    d_resid = cot + normalise_back(d_normed2 * gain2, hat2, inv2)
    d_att = d_resid.astype(BF)
    proj_grad = nt(ctx_ref[...], d_att).astype(BF)
    put_tiles(grads0, ROWS[0], 12 * C, proj_grad[:, C - LANES:])
    gain_rows = jnp.concatenate([gain2_grad[:, 0:LANES], gain2_grad[:, C - LANES:], jnp.zeros((62, LANES), F32)], axis=0)
    put_tiles(grads0, ROWS[0], 13 * C, gain_rows.astype(BF))
    sum0.start_core()
    mixed = (resid + nn(fc2_w[...], act)).astype(BF)
    mixed_copies = trail(mixed, 0, mixed_out)
    dctx_ref[...] = nn(proj_w[...], d_att).astype(BF)

    for w in range(NW):
        if w == 2:
            sum0.start()
        rows = slice(w * TW, (w + 1) * TW)
        dblk = (nn(dctx_ref[:, rows], expand[...]) * mask).astype(BF)
        probs = p_ref[w]
        d_probs = nn(kv_ref[rows, C:], dblk)
        weighted = probs * d_probs
        d_scores = weighted - probs * jnp.sum(weighted, axis=0, keepdims=True)
        d_low = d_scores.astype(BF)
        dproj_ref[2 * C:, rows] = nt(dblk, probs.astype(BF)).astype(BF)
        dproj_ref[C:2 * C, rows] = nt(qblk_ref[w], d_low).astype(BF)
        d_q = (nn(k_ref[:, rows], d_low) * (mask * scaling)).astype(BF)
        dproj_ref[0:C, rows] = nt(d_q, expand[...]).astype(BF)
        p_ref[w] = d_scores

    dproj = dproj_ref[...]
    qkv_grad = nt(normed1, dproj).astype(BF)
    d_win = nn(qkv_w[...], dproj).astype(BF).astype(F32)
    gain1_grad = row_of(jnp.sum(d_win * hat1, axis=1, keepdims=True))
    for k in range(4):
        put_tiles(grads1, ROWS[1], k * C, qkv_grad[:, k * LANES:(k + 1) * LANES])
    put_tiles(grads1, ROWS[1], 4 * C, jnp.concatenate([qkv_grad[:, 4 * LANES:], proj_grad[:, 0:64]], axis=1))
    gain_rows = jnp.concatenate([gain1_grad[:, 0:LANES], gain1_grad[:, C - LANES:], jnp.zeros((62, LANES), F32)], axis=0)
    put_tiles(grads1, ROWS[1], 5 * C, gain_rows.astype(BF))
    sum1.start_core()

    for w in range(NW):
        z_ref[...] = jnp.zeros_like(z_ref)
        for cs in range(WC):
            at = slice((11 - cs) * HEADS * A, (11 - cs) * HEADS * A + HT)
            z_ref[0:A, at] += p_ref[w, cs * A:(cs + 1) * A, :]
        dz = z_ref[...]
        spread = jnp.concatenate([dz * entry[a:a + 1] for a in range(A)], axis=0).astype(BF)
        d_table = nt(nt(rep[...], spread).astype(BF), pair[...]).astype(BF)
        for k in range(3):
            grads_t[3 * w + k] = d_table[TROWS * k:TROWS * (k + 1), 0:LANES]
            grads_t[12 + k, :, 16 * w:16 * w + 16] = d_table[TROWS * k:TROWS * (k + 1), LANES:]
        if w == 1:
            sum1.start()
    for k in range(3):
        grads_t[12 + k, :, 64:] = jnp.zeros((TROWS, 64), BF)
    grads_t[15] = jnp.zeros((TROWS, LANES), BF)
    sum_t.start()

    d_field = (d_resid + normalise_back(d_win * gain1, hat1, inv1)).astype(BF)
    fgrad_copies = trail(d_field, 1, fgrad_out)
    sum0.across()
    sum1.across()
    sum0.back()
    sum_t.across()
    sum1.back()
    sum_t.back()
    sum0.finish()
    sum1.finish()
    sum_t.finish()
    sum0.finish_core()
    sum1.finish_core()
    for each in (sum0, sum1, sum_t):
        each.finish_sends()
    for copy in mixed_copies + fgrad_copies:
        copy.wait()


def results_kernel(
    mixed_in, fgrad_in, final0, final1, final_t,
    mixed, fgrad, qkv, proj, fc1, fc2, gain_attn, gain_mlp, table, sems,
):
    outward = [pltpu.make_async_copy(a, b, sems.at[k]) for k, (a, b) in enumerate(((mixed_in, mixed), (fgrad_in, fgrad)))]
    for copy in outward:
        copy.start()
    for k in range(6):
        fc1[:, k * LANES:(k + 1) * LANES] = get_tiles(final0, ROWS[0], k * C, C)
        fc2[:, k * LANES:(k + 1) * LANES] = get_tiles(final0, ROWS[0], (6 + k) * C, C)
    proj[:, 64:] = get_tiles(final0, ROWS[0], 12 * C, C)
    for k in range(4):
        qkv[:, k * LANES:(k + 1) * LANES] = get_tiles(final1, ROWS[1], k * C, C)
    shared = get_tiles(final1, ROWS[1], 4 * C, C)
    qkv[:, 4 * LANES:] = shared[:, 0:64]
    proj[:, 0:64] = shared[:, 64:]
    for out, final, row in ((gain_attn, final1, 5 * C), (gain_mlp, final0, 13 * C)):
        rows = get_tiles(final, final.shape[1], row, 16)
        out[:, 0:LANES] = rows[0:1]
        out[:, LANES:] = rows[1:2, 64:]
    for w in range(NW):
        wide = jnp.concatenate([final_t[3 * w + k].astype(F32) for k in range(3)], axis=0)
        tail = jnp.concatenate([final_t[12 + k].astype(F32) for k in range(3)], axis=0)
        for h in range(HEADS):
            table[w, h, :, 0, 0:LANES] = wide[h * RELP:h * RELP + REL]
            table[w, h, :, 0, LANES:] = tail[h * RELP:h * RELP + REL, 16 * w:16 * w + 16]
    for copy in outward:
        copy.wait()


def shards(field, cotangent, gain_attn, gain_mlp, qkv_weight, proj_weight, fc1_weight, fc2_weight, bias_table):
    consts = [jnp.asarray(v) for v in constants()]
    sds = jax.ShapeDtypeStruct
    vm = pl.BlockSpec(memory_space=pltpu.VMEM)
    hbm = pl.BlockSpec(memory_space=pl.ANY)
    levels, rows, flat = field.shape
    tile = (rows, levels, flat)
    dma = pltpu.SemaphoreType.DMA
    operands = [
        field.transpose(1, 0, 2), cotangent.transpose(1, 0, 2), gain_attn.reshape(1, C), gain_mlp.reshape(1, C),
        qkv_weight, proj_weight, fc1_weight, fc2_weight.T, bias_table.transpose(0, 2, 3, 1, 4), *consts,
    ]
    pieces = pl.pallas_call(
        block_kernel,
        out_shape=(
            sds(tile, BF), sds(tile, BF),
            sds((2 * PEERS, ROWS[0], LANES), BF), sds((2 * PEERS, ROWS[1], LANES), BF), sds((PEERS, TROWS, LANES), BF),
        ),
        in_specs=[hbm] * len(operands),
        out_specs=(vm,) * 5,
        scratch_shapes=[pltpu.VMEM(v.shape, v.dtype) for v in operands[2:]] + [
            pltpu.VMEM((TOK, C), F32),
            pltpu.VMEM((HEADS * RELP, TW), F32),
            pltpu.VMEM((NW, TW, HT), F32),
            pltpu.VMEM((16, ZL), F32),
            pltpu.VMEM((NW, TW, HT), F32),
            pltpu.VMEM((NW, C, HT), BF),
            pltpu.VMEM((C, TOK), BF), pltpu.VMEM((C, TOK), BF), pltpu.VMEM((C, TOK), BF),
            pltpu.VMEM((TOK, 2 * C), BF),
            pltpu.VMEM((C, TOK), BF), pltpu.VMEM((C, TOK), BF),
            pltpu.VMEM((3 * C, TOK), BF),
            pltpu.VMEM((2,) + tile, BF),
            pltpu.VMEM((2,) + tile, BF),
            pltpu.VMEM((2 * PEERS, ROWS[0], LANES), BF), pltpu.VMEM((2 * PEERS, ROWS[1], LANES), BF), pltpu.VMEM((PEERS, TROWS, LANES), BF),
            pltpu.VMEM((PEERS, ROWS[0], LANES), BF), pltpu.VMEM((PEERS, ROWS[1], LANES), BF),
            pltpu.VMEM((PEERS, ROWS[0], LANES), BF), pltpu.VMEM((PEERS, ROWS[1], LANES), BF),
            pltpu.VMEM((PEERS, ROWS[0], LANES), BF), pltpu.VMEM((PEERS, ROWS[1], LANES), BF), pltpu.VMEM((PEERS, TROWS, LANES), BF),
            pltpu.VMEM((2, ROWS[0], LANES), BF), pltpu.VMEM((2, ROWS[1], LANES), BF), pltpu.VMEM((2, TROWS, LANES), BF),
            pltpu.VMEM((4, ROWS[0], LANES), BF), pltpu.VMEM((4, ROWS[1], LANES), BF), pltpu.VMEM((2, TROWS, LANES), BF),
            dma((len(operands) - 2,)), dma((7,)), dma((6,)), dma((6,)), dma((6,)), dma((6,)), dma((2, 2)), dma((2, 2)),
            dma((3, 3)), dma((3, 3)),
        ],
        compiler_params=pltpu.CompilerParams(vmem_limit_bytes=36 * 1024 * 1024, collective_id=0, has_side_effects=True),
        name="block",
    )(
        *[pltpu.with_memory_space_constraint(v, pltpu.HBM) for v in operands]
    )
    mixed, fgrad, qkv, proj, fc1, fc2, gain1, gain2, table = pl.pallas_call(
        results_kernel,
        out_shape=(
            sds(tile, BF), sds(tile, BF), sds((C, 3 * C), F32), sds((C, C), F32), sds((C, HID), F32), sds((C, HID), F32),
            sds((1, C), F32), sds((1, C), F32), sds((NW, HEADS, REL, 1, TW), F32),
        ),
        in_specs=[vm] * 5,
        out_specs=(hbm,) * 2 + (vm,) * 7,
        scratch_shapes=[dma((2,))],
        compiler_params=pltpu.CompilerParams(vmem_limit_bytes=16 * 1024 * 1024),
        name="results",
    )(*pieces)
    return (
        mixed.transpose(1, 0, 2), fgrad.transpose(1, 0, 2), qkv, proj, fc1, fc2.T,
        gain1.reshape(C), gain2.reshape(C), table.transpose(0, 3, 1, 2, 4),
    )


def solution(mesh):
    grid = P(None, "lat", "lon")
    by_type = P(None, "lat", None, None, None)
    return jax.shard_map(
        shards,
        mesh=mesh,
        in_specs=(grid, grid) + (P(),) * 6 + (by_type,),
        out_specs=(grid, grid) + (P(),) * 6 + (by_type,),
        check_vma=False,
    )
```

```python
import functools
import jax
import jax.numpy as jnp
import numpy as np
from jax import lax
from jax.experimental import pallas as pl
from jax.experimental.pallas import tpu as pltpu
from jax.sharding import PartitionSpec as P

BF = jnp.bfloat16
F32 = jnp.float32
C = 192
HEADS = 6
HEAD = 32
HID = 768
WZ, WR, WC = 2, 6, 12
A = WZ * WR
TW = A * WC
NW = 4
TOK = NW * TW
REL = 2 * WC - 1
RELP = 24
HT = HEADS * TW
ZL = REL * HEADS * A
EPS = 1e-05
MASKED = -1000000000.0


def constants():
    perm = np.zeros((WC, WR, 8, NW, WC, WZ, WR), np.float32)
    for c in range(WC):
        for w in range(NW):
            for lev in range(WZ):
                for r in range(WR):
                    perm[c, r, (2 * w + lev + 1) % 8, w, c, lev, r] = 1
    perm = perm.reshape(TOK, TOK)
    expand = np.zeros((WC, A, WC, HEADS, A), np.float32)
    for c in range(WC):
        for a in range(A):
            expand[c, a, c, :, a] = 1
    expand = expand.reshape(TW, HT)
    head_mask = np.zeros((HEADS, HEAD, WC, HEADS, A), np.float32)
    for h in range(HEADS):
        head_mask[h, :, :, h, :] = 1
    head_mask = head_mask.reshape(C, HT)
    rep = np.zeros((HEADS, RELP, REL, HEADS, A), np.float32)
    for h in range(HEADS):
        for rel in range(REL):
            rep[h, rel, rel, h, :] = 1
    rep = np.concatenate([rep.reshape(HEADS * RELP, ZL)] * 3)
    pair = np.zeros((WZ, WZ, WR, WR, WZ, WR, 16), np.float32)
    for lt in range(WZ):
        for ls in range(WZ):
            for rt in range(WR):
                for rs in range(WR):
                    pair[lt, ls, rt, rs, lt, rt, ls * WR + rs] = 1
    pair = pair.reshape(TW, A * 16)
    lane_a = np.arange(ZL) % A
    entry = (np.arange(A)[:, None] == lane_a[None, :]).astype(np.float32)
    entry = np.concatenate([entry, np.zeros((4, ZL), np.float32)])
    b = np.arange(16)
    level_differs = ((b[:, None] // WR) != (lane_a[None, :] // WR)) & (b[:, None] < A)
    row_differs = ((b[:, None] % WR >= 3) != (lane_a[None, :] % WR >= 3)) & (b[:, None] < A)
    differs = np.stack([level_differs, row_differs]).astype(np.float32)
    return [np.asarray(v, dtype=BF) for v in (perm, expand, head_mask, rep, pair)] + [entry, differs]


def nn(a, b):
    return lax.dot_general(a, b, (((1,), (0,)), ((), ())), preferred_element_type=F32)


def nt(a, b):
    return lax.dot_general(a, b, (((1,), (1,)), ((), ())), preferred_element_type=F32)


def tn(a, b):
    return lax.dot_general(a, b, (((0,), (0,)), ((), ())), preferred_element_type=F32)


def column_of(row):
    size = row.shape[1]
    eye = lax.broadcasted_iota(jnp.int32, (size, size), 0) == lax.broadcasted_iota(jnp.int32, (size, size), 1)
    return jnp.sum(jnp.where(eye, row, 0.0), axis=1, keepdims=True)


def row_of(column):
    size = column.shape[0]
    eye = lax.broadcasted_iota(jnp.int32, (size, size), 0) == lax.broadcasted_iota(jnp.int32, (size, size), 1)
    return jnp.sum(jnp.where(eye, column, 0.0), axis=0, keepdims=True)


def normalise(v):
    centre = v - jnp.sum(v, axis=0, keepdims=True) * (1.0 / C)
    inv = lax.rsqrt(jnp.sum(centre * centre, axis=0, keepdims=True) * (1.0 / C) + EPS)
    return centre * inv, inv


def normalise_back(g, hat, inv):
    return inv * (g - jnp.sum(g, axis=0, keepdims=True) * (1.0 / C) - hat * (jnp.sum(g * hat, axis=0, keepdims=True) * (1.0 / C)))


def tokens_of(x_ref, win):
    for c in range(WC):
        x_ref[c * 48:(c + 1) * 48, :] = win[:, :, c * C:(c + 1) * C].astype(F32).reshape(48, C)
    return x_ref[...].astype(BF)


HALF = WC * C // 2
LANES = 128
PEERS = 16
ROWS = (80, 32)
TROWS = 48
MESH_ID = pl.DeviceIdType.MESH


def place():
    lon, lat = lax.axis_index("lon"), lax.axis_index("lat")
    return (lon // 4) % 2 * 2 + lat // 2, lon // 8, lon % 4, lat % 2


def device_at(x, y, z, core):
    return ((y * 2 + x // 2) * 4 + z, x % 2 * 2 + core)


def remote(src, dst, send_sem, recv_sem, device):
    return pltpu.make_async_remote_copy(
        src_ref=src, dst_ref=dst, send_sem=send_sem, recv_sem=recv_sem, device_id=device, device_id_type=MESH_ID
    )


def drain(like, sem):
    pltpu.make_async_copy(like, like, sem).wait()


def total(ref, count):
    value = ref[0].astype(F32)
    for k in range(1, count):
        value = value + ref[k].astype(F32)
    return value.astype(BF)


class PlaneSum:
    def __init__(self, axes, piece, terms, part, cross, final, sends, recvs):
        self.axes, self.piece, self.terms, self.part, self.cross, self.final = axes, piece, terms, part, cross, final
        self.sends, self.recvs = sends, recvs
        self.at = place()
        self.me = self.at[axes[0]] * 4 + self.at[axes[1]]
        self.count = cross.shape[0]
        self.step = 4 // self.count
        self.mine = self.at[axes[2]] // self.step
        self.others = terms.at[pl.ds(1, PEERS - 1)]
        self.few = cross.at[pl.ds(1, self.count - 1)]

    def in_plane(self, s):
        p = (self.me + s) % PEERS
        at = list(self.at)
        at[self.axes[0]], at[self.axes[1]] = p // 4, p % 4
        return p, device_at(*at)

    def along(self, s):
        at = list(self.at)
        at[self.axes[2]] = (at[self.axes[2]] + s * self.step) % 4
        return device_at(*at)

    def start(self):
        for s in range(1, PEERS):
            p, device = self.in_plane(s)
            remote(self.piece(p), self.terms.at[s], self.sends.at[0], self.recvs.at[0], device).start()

    def across(self):
        self.terms[0] = self.piece(self.me)[...]
        drain(self.others, self.recvs.at[0])
        value = total(self.terms, PEERS)
        self.part[0] = value
        self.cross[self.mine] = value
        for s in range(1, self.count):
            remote(self.part.at[0], self.cross.at[self.mine], self.sends.at[1], self.recvs.at[1], self.along(s)).start()

    def back(self):
        drain(self.few, self.recvs.at[1])
        value = total(self.cross, self.count)
        self.part[1] = value
        self.final[self.first + self.me] = value
        for s in range(1, PEERS):
            remote(self.part.at[1], self.final.at[self.first + self.me], self.sends.at[2], self.recvs.at[2], self.in_plane(s)[1]).start()

    def finish(self):
        drain(self.others, self.recvs.at[2])

    def finish_sends(self):
        drain(self.others, self.sends.at[0])
        drain(self.few, self.sends.at[1])
        drain(self.others, self.sends.at[2])

    first = 0


class CoreSum(PlaneSum):
    def __init__(self, axes, grads, got, halves, final, core_sems, *args):
        self.grads, self.got, self.halves, self.core_sems = grads, got, halves, core_sems
        super().__init__(axes, lambda p: halves.at[p], *args[:3], final, *args[3:])
        self.core = self.at[3]
        self.first = self.core * PEERS
        self.other = device_at(*self.at[:3], 1 - self.core)

    def start_core(self):
        self.swap = remote(self.grads.at[pl.ds((1 - self.core) * PEERS, PEERS)], self.got, self.core_sems[0].at[0], self.core_sems[1].at[0], self.other)
        self.swap.start()

    def start(self):
        self.swap.wait()
        for p in range(PEERS):
            self.halves[p] = (self.grads[self.core * PEERS + p].astype(F32) + self.got[p].astype(F32)).astype(BF)
        super().start()

    def finish(self):
        super().finish()
        mine = self.final.at[pl.ds(self.first, PEERS)]
        self.swap = remote(mine, mine, self.core_sems[0].at[1], self.core_sems[1].at[1], self.other)
        self.swap.start()

    def finish_core(self):
        self.swap.wait()


def put_tiles(ref, rows, first, value):
    done = 0
    while done < value.shape[0]:
        piece, row = divmod(first + done, rows)
        count = min(rows - row, value.shape[0] - done)
        ref[piece, row:row + count, :] = value[done:done + count]
        done += count


def get_tiles(ref, rows, first, count):
    parts, done = [], 0
    while done < count:
        piece, row = divmod(first + done, rows)
        take = min(rows - row, count - done)
        parts.append(ref[piece, row:row + take, :].astype(F32))
        done += take
    return parts[0] if len(parts) == 1 else jnp.concatenate(parts, axis=0)


def block_kernel(
    field_ref, cot_ref, *refs,
):
    count = 14
    sources, outs, (held, rest) = refs[:count], refs[count:count + 5], (refs[count + 5:2 * count + 5], refs[2 * count + 5:])
    block(field_ref, cot_ref, sources, held, *outs, *rest)


def block(
    field_ref, cot_ref, sources, held,
    mixed_out, fgrad_out, final0, final1, final_t,
    x_ref, t_ref, bias_ref, z_ref, p_ref, qblk_ref, q_ref, k_ref, v_ref, kv_ref, ctx_ref, dctx_ref, dproj_ref,
    win_ref, send_ref, grads0, grads1, grads_t, got0, got1, halves0, halves1,
    terms0, terms1, terms_t, part0, part1, part_t, cross0, cross1, cross_t,
    load_sems, local_sems, halo_send, halo_recv, trail_send, trail_recv, core_send, core_recv,
    sum_send, sum_recv, ready,
):
    gain_attn, gain_mlp, qkv_w, proj_w, fc1_w, fc2_w, table, perm, expand, head_mask, rep, pair, entry, differs = held
    lon, lat = lax.axis_index("lon"), lax.axis_index("lat")
    lon_n, lat_n = 32, 4
    west, east = (lon + lon_n - 1) % lon_n, (lon + 1) % lon_n
    above, below = (lat + lat_n - 1) % lat_n, (lat + 1) % lat_n

    sum0, sum1 = [
        CoreSum((0, 1, 2), grads, got, halves, final, (core_send.at[k], core_recv.at[k]), terms, part, cross, sum_send.at[k], sum_recv.at[k])
        for k, (grads, got, halves, final, terms, part, cross) in enumerate((
            (grads0, got0, halves0, final0, terms0, part0, cross0), (grads1, got1, halves1, final1, terms1, part1, cross1),
        ))
    ]
    sum_t = PlaneSum((1, 2, 0), lambda p: grads_t.at[p], terms_t, part_t, cross_t, final_t, sum_send.at[2], sum_recv.at[2])

    barrier = pltpu.get_barrier_semaphore()
    partners = [(west, lat), (east, lat), (lon, above), (lon, below), (west, above), (east, below)]
    chip = list(place())
    lines = []
    for axis in range(3):
        for s in range(1, 4):
            at = list(chip)
            at[axis] = (at[axis] + s) % 4
            lines.append(device_at(*at))
    partners += [sum0.other] + lines
    for device in partners:
        pl.semaphore_signal(barrier, inc=1, device_id=device, device_id_type=MESH_ID)
    loads = [pltpu.make_async_copy(a, b, load_sems.at[k]) for k, (a, b) in enumerate(zip(sources, held))]
    first = (6, 11, 10, 12, 13)
    for k in first:
        loads[k].start()
    pl.semaphore_wait(barrier, len(partners))

    right, left = pl.ds(HALF, HALF), pl.ds(0, HALF)
    upper, lower = pl.ds(0, 3), pl.ds(3, 3)
    halos = []
    for k, source in enumerate((field_ref, cot_ref)):
        win = win_ref.at[k]
        copies = [pltpu.make_async_copy(source.at[lower, :, right], win.at[upper, :, left], local_sems.at[k])]
        for s, (rows, cols, device) in enumerate((((lower, upper), (left, right), (west, lat)), ((upper, lower), (right, left), (lon, above)), ((upper, lower), (left, right), (west, above)))):
            copies.append(remote(source.at[rows[0], :, cols[0]], win.at[rows[1], :, cols[1]], halo_send.at[3 * k + s], halo_recv.at[3 * k + s], device))
        halos.append(copies)
    for copy in halos[0]:
        copy.start()
    for k in range(len(loads)):
        if k not in first:
            loads[k].start()

    def trail(value, k, out):
        win = send_ref.at[k]
        back = nt(perm[...], value)
        for c in range(WC):
            win[:, :, c * C:(c + 1) * C] = back[c * 48:(c + 1) * 48].reshape(WR, 8, C).astype(BF)
        copies = [pltpu.make_async_copy(win.at[upper, :, left], out.at[lower, :, right], local_sems.at[2 + k])]
        for s, (rows, cols, device) in enumerate((((upper, lower), (right, left), (east, lat)), ((lower, upper), (left, right), (lon, below)), ((lower, upper), (right, left), (east, below)))):
            copies.append(remote(win.at[rows[0], :, cols[0]], out.at[rows[1], :, cols[1]], trail_send.at[3 * k + s], trail_recv.at[3 * k + s], device))
        for copy in copies:
            copy.start()
        return copies

    for k in first:
        loads[k].wait()
    for device in lines:
        pl.semaphore_signal(ready, inc=1, device_id=device, device_id_type=MESH_ID)

    t_ref[...] = jnp.zeros_like(t_ref)
    for w in range(NW):
        for h in range(HEADS):
            t_ref[h * RELP:h * RELP + REL, :] = table[w, h, :, 0, :]
        rest = t_ref[...]
        moved = []
        for part in range(3):
            low = rest.astype(BF)
            rest = rest - low.astype(F32)
            moved.append(nn(low, pair[...]).astype(BF))
        spread = tn(jnp.concatenate(moved, axis=0), rep[...])
        z = spread[0:16] * entry[0:1]
        for a in range(1, A):
            z = z + spread[16 * a:16 * a + 16] * entry[a:a + 1]
        hide = jnp.where(lat == lat_n - 1, differs[1], 0.0)
        if w == NW - 1:
            hide = hide + differs[0]
        z = jnp.where(hide > 0.5, MASKED, z)
        for cs in range(WC):
            bias_ref[w, cs * A:(cs + 1) * A, :] = z[0:A, (11 - cs) * HEADS * A:(11 - cs) * HEADS * A + HT]

    for k in range(len(loads)):
        if k not in first:
            loads[k].wait()
    for copy in halos[0]:
        copy.wait()
    for copy in halos[1]:
        copy.start()
    field = tn(tokens_of(x_ref, win_ref.at[0]), perm[...])

    gain1 = column_of(gain_attn[...])
    gain2 = column_of(gain_mlp[...])
    hat1, inv1 = normalise(field)
    normed1 = (hat1 * gain1).astype(BF)
    projected = tn(qkv_w[...], normed1)
    scaling = HEAD ** (-0.5)
    q_ref[...] = (projected[0:C] * scaling).astype(BF)
    k_ref[...] = projected[C:2 * C].astype(BF)
    v_ref[...] = projected[2 * C:].astype(BF)
    kv_ref[...] = tn(normed1, qkv_w[:, C:]).astype(BF)
    mask = head_mask[...]

    for w in range(NW):
        rows = slice(w * TW, (w + 1) * TW)
        qblk = nn(q_ref[:, rows], expand[...]).astype(BF) * mask
        qblk_ref[w] = qblk
        scores = nn(kv_ref[rows, 0:C], qblk) + bias_ref[w]
        raised = jnp.exp(scores - jnp.max(scores, axis=0, keepdims=True))
        probs = raised * (1.0 / jnp.sum(raised, axis=0, keepdims=True))
        p_ref[w] = probs
        context = nn(v_ref[:, rows], probs.astype(BF)).astype(BF) * mask
        ctx_ref[:, rows] = nt(context, expand[...]).astype(BF)
    attended = tn(proj_w[...], ctx_ref[...]).astype(BF)

    for copy in halos[1]:
        copy.wait()
    cot = tn(tokens_of(x_ref, win_ref.at[1]), perm[...])
    cot_low = cot.astype(BF)

    resid = field + attended.astype(F32)
    hat2, inv2 = normalise(resid)
    normed2 = (hat2 * gain2).astype(BF)
    hidden = tn(fc1_w[...], normed2)
    k0 = 0.7978845608028654
    k1 = 0.044715
    sq = hidden * hidden
    th = jnp.tanh(hidden * (k0 + (k0 * k1) * sq))
    half = 0.5 * (1.0 + th)
    act = (hidden * half).astype(BF)
    slope = half + 0.5 * hidden * (1.0 - th * th) * (k0 + (3.0 * k0 * k1) * sq)
    d_act = tn(fc2_w[...], cot_low).astype(BF)
    d_pre = (d_act.astype(F32) * slope).astype(BF)
    fc1_grad = nt(normed2, d_pre).astype(BF)
    fc2_grad = nt(cot_low, act).astype(BF)
    for k in range(6):
        put_tiles(grads0, ROWS[0], k * C, fc1_grad[:, k * LANES:(k + 1) * LANES])
        put_tiles(grads0, ROWS[0], (6 + k) * C, fc2_grad[:, k * LANES:(k + 1) * LANES])
    d_normed2 = nn(fc1_w[...], d_pre)
    gain2_grad = row_of(jnp.sum(d_normed2 * hat2, axis=1, keepdims=True))
    d_resid = cot + normalise_back(d_normed2 * gain2, hat2, inv2)
    d_att = d_resid.astype(BF)
    proj_grad = nt(ctx_ref[...], d_att).astype(BF)
    put_tiles(grads0, ROWS[0], 12 * C, proj_grad[:, C - LANES:])
    gain_rows = jnp.concatenate([gain2_grad[:, 0:LANES], gain2_grad[:, C - LANES:], jnp.zeros((62, LANES), F32)], axis=0)
    put_tiles(grads0, ROWS[0], 13 * C, gain_rows.astype(BF))
    sum0.start_core()
    mixed = (resid + nn(fc2_w[...], act)).astype(BF)
    mixed_copies = trail(mixed, 0, mixed_out)
    dctx_ref[...] = nn(proj_w[...], d_att).astype(BF)

    for w in range(NW):
        if w == 1:
            pl.semaphore_wait(ready, len(lines))
            sum0.start()
        rows = slice(w * TW, (w + 1) * TW)
        dblk = nn(dctx_ref[:, rows], expand[...]).astype(BF) * mask
        probs = p_ref[w]
        d_probs = nn(kv_ref[rows, C:], dblk)
        weighted = probs * d_probs
        d_scores = weighted - probs * jnp.sum(weighted, axis=0, keepdims=True)
        d_low = d_scores.astype(BF)
        dproj_ref[2 * C:, rows] = nt(dblk, probs.astype(BF)).astype(BF)
        dproj_ref[C:2 * C, rows] = nt(qblk_ref[w], d_low).astype(BF)
        d_q = (nn(k_ref[:, rows], d_low) * scaling).astype(BF) * mask
        dproj_ref[0:C, rows] = nt(d_q, expand[...]).astype(BF)
        p_ref[w] = d_scores

    dproj = dproj_ref[...]
    qkv_grad = nt(normed1, dproj).astype(BF)
    d_win = nn(qkv_w[...], dproj).astype(BF).astype(F32)
    gain1_grad = row_of(jnp.sum(d_win * hat1, axis=1, keepdims=True))
    for k in range(4):
        put_tiles(grads1, ROWS[1], k * C, qkv_grad[:, k * LANES:(k + 1) * LANES])
    put_tiles(grads1, ROWS[1], 4 * C, jnp.concatenate([qkv_grad[:, 4 * LANES:], proj_grad[:, 0:64]], axis=1))
    gain_rows = jnp.concatenate([gain1_grad[:, 0:LANES], gain1_grad[:, C - LANES:], jnp.zeros((62, LANES), F32)], axis=0)
    put_tiles(grads1, ROWS[1], 5 * C, gain_rows.astype(BF))
    sum1.start_core()

    for w in range(NW):
        z_ref[...] = jnp.zeros_like(z_ref)
        for cs in range(WC):
            at = slice((11 - cs) * HEADS * A, (11 - cs) * HEADS * A + HT)
            z_ref[0:A, at] += p_ref[w, cs * A:(cs + 1) * A, :]
        dz = z_ref[...]
        spread = jnp.concatenate([dz * entry[a:a + 1] for a in range(A)], axis=0).astype(BF)
        d_table = nt(nt(rep[0:HEADS * RELP, :], spread).astype(BF), pair[...]).astype(BF)
        for k in range(3):
            grads_t[3 * w + k] = d_table[TROWS * k:TROWS * (k + 1), 0:LANES]
            grads_t[12 + k, :, 16 * w:16 * w + 16] = d_table[TROWS * k:TROWS * (k + 1), LANES:]
        if w == 1:
            sum1.start()
    for k in range(3):
        grads_t[12 + k, :, 64:] = jnp.zeros((TROWS, 64), BF)
    grads_t[15] = jnp.zeros((TROWS, LANES), BF)
    sum_t.start()

    d_field = (d_resid + normalise_back(d_win * gain1, hat1, inv1)).astype(BF)
    fgrad_copies = trail(d_field, 1, fgrad_out)
    sum0.across()
    sum1.across()
    sum_t.across()
    sum1.back()
    sum0.back()
    sum_t.back()
    sum1.finish()
    sum0.finish()
    sum_t.finish()
    sum1.finish_core()
    sum0.finish_core()
    for each in (sum0, sum1, sum_t):
        each.finish_sends()
    for copy in mixed_copies + fgrad_copies:
        copy.wait()


def results_kernel(
    mixed_in, fgrad_in, final0, final1, final_t,
    mixed_out, fgrad_out, qkv_out, proj_out, fc1_out, fc2_out, gain_attn_out, gain_mlp_out, table_out,
    qkv, proj, fc1, fc2, gain_attn, gain_mlp, table, sems,
):
    outward = []

    def send(value, out):
        outward.append(pltpu.make_async_copy(value, out, sems.at[len(outward)]))
        outward[-1].start()

    send(mixed_in, mixed_out)
    send(fgrad_in, fgrad_out)
    for w in range(NW):
        wide = jnp.concatenate([final_t[3 * w + k].astype(F32) for k in range(3)], axis=0)
        tail = jnp.concatenate([final_t[12 + k].astype(F32) for k in range(3)], axis=0)
        for h in range(HEADS):
            table[w, h, :, 0, 0:LANES] = wide[h * RELP:h * RELP + REL]
            table[w, h, :, 0, LANES:] = tail[h * RELP:h * RELP + REL, 16 * w:16 * w + 16]
    send(table, table_out)
    for k in range(6):
        fc1[:, k * LANES:(k + 1) * LANES] = get_tiles(final0, ROWS[0], k * C, C)
    send(fc1, fc1_out)
    for k in range(6):
        fc2[:, k * LANES:(k + 1) * LANES] = get_tiles(final0, ROWS[0], (6 + k) * C, C)
    send(fc2, fc2_out)
    proj[:, 64:] = get_tiles(final0, ROWS[0], 12 * C, C)
    for k in range(4):
        qkv[:, k * LANES:(k + 1) * LANES] = get_tiles(final1, ROWS[1], k * C, C)
    shared = get_tiles(final1, ROWS[1], 4 * C, C)
    qkv[:, 4 * LANES:] = shared[:, 0:64]
    proj[:, 0:64] = shared[:, 64:]
    send(qkv, qkv_out)
    send(proj, proj_out)
    for gain, out, final, row in ((gain_attn, gain_attn_out, final1, 5 * C), (gain_mlp, gain_mlp_out, final0, 13 * C)):
        rows = get_tiles(final, final.shape[1], row, 16)
        gain[:, 0:LANES] = rows[0:1]
        gain[:, LANES:] = rows[1:2, 64:]
        send(gain, out)
    for copy in outward:
        copy.wait()


def shards(field, cotangent, gain_attn, gain_mlp, qkv_weight, proj_weight, fc1_weight, fc2_weight, bias_table):
    consts = [jnp.asarray(v) for v in constants()]
    sds = jax.ShapeDtypeStruct
    vm = pl.BlockSpec(memory_space=pltpu.VMEM)
    hbm = pl.BlockSpec(memory_space=pl.ANY)
    levels, rows, flat = field.shape
    tile = (rows, levels, flat)
    dma = pltpu.SemaphoreType.DMA
    operands = [
        field.transpose(1, 0, 2), cotangent.transpose(1, 0, 2), gain_attn.reshape(1, C), gain_mlp.reshape(1, C),
        qkv_weight, proj_weight, fc1_weight, fc2_weight.T, bias_table.transpose(0, 2, 3, 1, 4), *consts,
    ]
    pieces = pl.pallas_call(
        block_kernel,
        out_shape=(
            sds(tile, BF), sds(tile, BF),
            sds((2 * PEERS, ROWS[0], LANES), BF), sds((2 * PEERS, ROWS[1], LANES), BF), sds((PEERS, TROWS, LANES), BF),
        ),
        in_specs=[hbm] * len(operands),
        out_specs=(vm,) * 5,
        scratch_shapes=[pltpu.VMEM(v.shape, v.dtype) for v in operands[2:]] + [
            pltpu.VMEM((TOK, C), F32),
            pltpu.VMEM((HEADS * RELP, TW), F32),
            pltpu.VMEM((NW, TW, HT), F32),
            pltpu.VMEM((16, ZL), F32),
            pltpu.VMEM((NW, TW, HT), F32),
            pltpu.VMEM((NW, C, HT), BF),
            pltpu.VMEM((C, TOK), BF), pltpu.VMEM((C, TOK), BF), pltpu.VMEM((C, TOK), BF),
            pltpu.VMEM((TOK, 2 * C), BF),
            pltpu.VMEM((C, TOK), BF), pltpu.VMEM((C, TOK), BF),
            pltpu.VMEM((3 * C, TOK), BF),
            pltpu.VMEM((2,) + tile, BF),
            pltpu.VMEM((2,) + tile, BF),
            pltpu.VMEM((2 * PEERS, ROWS[0], LANES), BF), pltpu.VMEM((2 * PEERS, ROWS[1], LANES), BF), pltpu.VMEM((PEERS, TROWS, LANES), BF),
            pltpu.VMEM((PEERS, ROWS[0], LANES), BF), pltpu.VMEM((PEERS, ROWS[1], LANES), BF),
            pltpu.VMEM((PEERS, ROWS[0], LANES), BF), pltpu.VMEM((PEERS, ROWS[1], LANES), BF),
            pltpu.VMEM((PEERS, ROWS[0], LANES), BF), pltpu.VMEM((PEERS, ROWS[1], LANES), BF), pltpu.VMEM((PEERS, TROWS, LANES), BF),
            pltpu.VMEM((2, ROWS[0], LANES), BF), pltpu.VMEM((2, ROWS[1], LANES), BF), pltpu.VMEM((2, TROWS, LANES), BF),
            pltpu.VMEM((4, ROWS[0], LANES), BF), pltpu.VMEM((4, ROWS[1], LANES), BF), pltpu.VMEM((2, TROWS, LANES), BF),
            dma((len(operands) - 2,)), dma((7,)), dma((6,)), dma((6,)), dma((6,)), dma((6,)), dma((2, 2)), dma((2, 2)),
            dma((3, 3)), dma((3, 3)), pltpu.SemaphoreType.REGULAR,
        ],
        compiler_params=pltpu.CompilerParams(vmem_limit_bytes=36 * 1024 * 1024, collective_id=0, has_side_effects=True),
        name="block",
    )(
        *[pltpu.with_memory_space_constraint(v, pltpu.HBM) for v in operands]
    )
    shapes = [(C, 3 * C), (C, C), (C, HID), (C, HID), (1, C), (1, C), (NW, HEADS, REL, 1, TW)]
    mixed, fgrad, qkv, proj, fc1, fc2, gain1, gain2, table = pl.pallas_call(
        results_kernel,
        out_shape=[sds(tile, BF)] * 2 + [sds(v, F32) for v in shapes],
        in_specs=[vm] * 5,
        out_specs=[hbm] * 9,
        scratch_shapes=[pltpu.VMEM(v, F32) for v in shapes] + [dma((9,))],
        compiler_params=pltpu.CompilerParams(vmem_limit_bytes=16 * 1024 * 1024),
        name="results",
    )(*pieces)
    return (
        mixed.transpose(1, 0, 2), fgrad.transpose(1, 0, 2), qkv, proj, fc1, fc2.T,
        gain1.reshape(C), gain2.reshape(C), table.transpose(0, 3, 1, 2, 4),
    )


def solution(mesh):
    grid = P(None, "lat", "lon")
    by_type = P(None, "lat", None, None, None)
    return jax.shard_map(
        shards,
        mesh=mesh,
        in_specs=(grid, grid) + (P(),) * 6 + (by_type,),
        out_specs=(grid, grid) + (P(),) * 6 + (by_type,),
        check_vma=False,
    )
```

```python
import functools
import jax
import jax.numpy as jnp
import numpy as np
from jax import lax
from jax.experimental import pallas as pl
from jax.experimental.pallas import tpu as pltpu
from jax.sharding import PartitionSpec as P

BF = jnp.bfloat16
F32 = jnp.float32
C = 192
HEADS = 6
HEAD = 32
HID = 768
WZ, WR, WC = 2, 6, 12
A = WZ * WR
TW = A * WC
NW = 4
TOK = NW * TW
REL = 2 * WC - 1
RELP = 24
HT = HEADS * TW
ZL = REL * HEADS * A
EPS = 1e-05
MASKED = -1000000000.0


def constants():
    perm = np.zeros((WC, WR, 8, NW, WC, WZ, WR), np.float32)
    for c in range(WC):
        for w in range(NW):
            for lev in range(WZ):
                for r in range(WR):
                    perm[c, r, (2 * w + lev + 1) % 8, w, c, lev, r] = 1
    perm = perm.reshape(TOK, TOK)
    rep = np.zeros((HEADS, RELP, HEADS, REL, A), np.float32)
    for h in range(HEADS):
        for rel in range(REL):
            rep[h, rel, h, rel, :] = 1
    rep = np.concatenate([rep.reshape(HEADS * RELP, ZL)] * 3)
    pair = np.zeros((WZ, WZ, WR, WR, WZ, WR, 16), np.float32)
    for lt in range(WZ):
        for ls in range(WZ):
            for rt in range(WR):
                for rs in range(WR):
                    pair[lt, ls, rt, rs, lt, rt, ls * WR + rs] = 1
    pair = pair.reshape(TW, A * 16)
    lane_a = np.arange(ZL) % A
    entry = (np.arange(A)[:, None] == lane_a[None, :]).astype(np.float32)
    entry = np.concatenate([entry, np.zeros((4, ZL), np.float32)])
    b = np.arange(16)
    level_differs = ((b[:, None] // WR) != (lane_a[None, :] // WR)) & (b[:, None] < A)
    row_differs = ((b[:, None] % WR >= 3) != (lane_a[None, :] % WR >= 3)) & (b[:, None] < A)
    differs = np.stack([level_differs, row_differs]).astype(np.float32)
    return [np.asarray(v, dtype=BF) for v in (perm, rep, pair)] + [entry, differs]


def nn(a, b):
    return lax.dot_general(a, b, (((1,), (0,)), ((), ())), preferred_element_type=F32)


def nt(a, b):
    return lax.dot_general(a, b, (((1,), (1,)), ((), ())), preferred_element_type=F32)


def tn(a, b):
    return lax.dot_general(a, b, (((0,), (0,)), ((), ())), preferred_element_type=F32)


def column_of(row):
    size = row.shape[1]
    eye = lax.broadcasted_iota(jnp.int32, (size, size), 0) == lax.broadcasted_iota(jnp.int32, (size, size), 1)
    return jnp.sum(jnp.where(eye, row, 0.0), axis=1, keepdims=True)


def row_of(column):
    size = column.shape[0]
    eye = lax.broadcasted_iota(jnp.int32, (size, size), 0) == lax.broadcasted_iota(jnp.int32, (size, size), 1)
    return jnp.sum(jnp.where(eye, column, 0.0), axis=0, keepdims=True)


def normalise(v):
    centre = v - jnp.sum(v, axis=0, keepdims=True) * (1.0 / C)
    inv = lax.rsqrt(jnp.sum(centre * centre, axis=0, keepdims=True) * (1.0 / C) + EPS)
    return centre * inv, inv


def normalise_back(g, hat, inv):
    return inv * (g - jnp.sum(g, axis=0, keepdims=True) * (1.0 / C) - hat * (jnp.sum(g * hat, axis=0, keepdims=True) * (1.0 / C)))


def tokens_of(x_ref, win):
    for c in range(WC):
        x_ref[c * 48:(c + 1) * 48, :] = win[:, :, c * C:(c + 1) * C].astype(F32).reshape(48, C)
    return x_ref[...].astype(BF)


HALF = WC * C // 2
LANES = 128
PEERS = 16
ROWS = (80, 32)
TROWS = 48
MESH_ID = pl.DeviceIdType.MESH


def place():
    lon, lat = lax.axis_index("lon"), lax.axis_index("lat")
    return (lon // 4) % 2 * 2 + lat // 2, lon // 8, lon % 4, lat % 2


def device_at(x, y, z, core):
    return ((y * 2 + x // 2) * 4 + z, x % 2 * 2 + core)


def remote(src, dst, send_sem, recv_sem, device):
    return pltpu.make_async_remote_copy(
        src_ref=src, dst_ref=dst, send_sem=send_sem, recv_sem=recv_sem, device_id=device, device_id_type=MESH_ID
    )


def drain(like, sem):
    pltpu.make_async_copy(like, like, sem).wait()


def total(ref, count):
    value = ref[0].astype(F32)
    for k in range(1, count):
        value = value + ref[k].astype(F32)
    return value.astype(BF)


class PlaneSum:
    def __init__(self, axes, piece, terms, part, cross, final, sends, recvs):
        self.axes, self.piece, self.terms, self.part, self.cross, self.final = axes, piece, terms, part, cross, final
        self.sends, self.recvs = sends, recvs
        self.at = place()
        self.me = self.at[axes[0]] * 4 + self.at[axes[1]]
        self.count = cross.shape[0]
        self.step = 4 // self.count
        self.mine = self.at[axes[2]] // self.step
        self.others = terms.at[pl.ds(1, PEERS - 1)]
        self.few = cross.at[pl.ds(1, self.count - 1)]

    def in_plane(self, s):
        p = (self.me + s) % PEERS
        at = list(self.at)
        at[self.axes[0]], at[self.axes[1]] = p // 4, p % 4
        return p, device_at(*at)

    def along(self, s):
        at = list(self.at)
        at[self.axes[2]] = (at[self.axes[2]] + s * self.step) % 4
        return device_at(*at)

    def start(self):
        for s in range(1, PEERS):
            p, device = self.in_plane(s)
            remote(self.piece(p), self.terms.at[s], self.sends.at[0], self.recvs.at[0], device).start()

    def across(self):
        self.terms[0] = self.piece(self.me)[...]
        drain(self.others, self.recvs.at[0])
        value = total(self.terms, PEERS)
        self.part[0] = value
        self.cross[self.mine] = value
        for s in range(1, self.count):
            remote(self.part.at[0], self.cross.at[self.mine], self.sends.at[1], self.recvs.at[1], self.along(s)).start()

    def back(self):
        drain(self.few, self.recvs.at[1])
        value = total(self.cross, self.count)
        self.part[1] = value
        self.final[self.first + self.me] = value
        for s in range(1, PEERS):
            remote(self.part.at[1], self.final.at[self.first + self.me], self.sends.at[2], self.recvs.at[2], self.in_plane(s)[1]).start()

    def finish(self):
        drain(self.others, self.recvs.at[2])

    def finish_sends(self):
        drain(self.others, self.sends.at[0])
        drain(self.few, self.sends.at[1])
        drain(self.others, self.sends.at[2])

    first = 0


class CoreSum(PlaneSum):
    def __init__(self, axes, grads, got, halves, final, core_sems, *args):
        self.grads, self.got, self.halves, self.core_sems = grads, got, halves, core_sems
        super().__init__(axes, lambda p: halves.at[p], *args[:3], final, *args[3:])
        self.core = self.at[3]
        self.first = self.core * PEERS
        self.other = device_at(*self.at[:3], 1 - self.core)

    def start_core(self):
        self.swap = remote(self.grads.at[pl.ds((1 - self.core) * PEERS, PEERS)], self.got, self.core_sems[0].at[0], self.core_sems[1].at[0], self.other)
        self.swap.start()

    def start(self):
        self.swap.wait()
        for p in range(PEERS):
            self.halves[p] = (self.grads[self.core * PEERS + p].astype(F32) + self.got[p].astype(F32)).astype(BF)
        super().start()

    def finish(self):
        super().finish()
        mine = self.final.at[pl.ds(self.first, PEERS)]
        self.swap = remote(mine, mine, self.core_sems[0].at[1], self.core_sems[1].at[1], self.other)
        self.swap.start()

    def finish_core(self):
        self.swap.wait()


def put_tiles(ref, rows, first, value):
    done = 0
    while done < value.shape[0]:
        piece, row = divmod(first + done, rows)
        count = min(rows - row, value.shape[0] - done)
        ref[piece, row:row + count, :] = value[done:done + count]
        done += count


def get_tiles(ref, rows, first, count):
    parts, done = [], 0
    while done < count:
        piece, row = divmod(first + done, rows)
        take = min(rows - row, count - done)
        parts.append(ref[piece, row:row + take, :].astype(F32))
        done += take
    return parts[0] if len(parts) == 1 else jnp.concatenate(parts, axis=0)


def block_kernel(
    field_ref, cot_ref, *refs,
):
    count = 12
    sources, outs, (held, rest) = refs[:count], refs[count:count + 5], (refs[count + 5:2 * count + 5], refs[2 * count + 5:])
    block(field_ref, cot_ref, sources, held, *outs, *rest)


def block(
    field_ref, cot_ref, sources, held,
    mixed_out, fgrad_out, final0, final1, final_t,
    x_ref, t_ref, bias_ref, z_ref, p_ref, qblk_ref, dblk_ref, q_ref, k_ref, v_ref, kv_ref, ctx_ref, dctx_ref, dproj_ref, qkv_t, proj_t, fc1_t, fc2_t,
    win_ref, send_ref, grads0, grads1, grads_t, got0, got1, halves0, halves1,
    terms0, terms1, terms_t, part0, part1, part_t, cross0, cross1, cross_t,
    load_sems, local_sems, halo_send, halo_recv, trail_send, trail_recv, core_send, core_recv,
    sum_send, sum_recv, ready,
):
    gain_attn, gain_mlp, qkv_w, proj_w, fc1_w, fc2_w, table, perm, rep, pair, entry, differs = held
    lon, lat = lax.axis_index("lon"), lax.axis_index("lat")
    lon_n, lat_n = 32, 4
    west, east = (lon + lon_n - 1) % lon_n, (lon + 1) % lon_n
    above, below = (lat + lat_n - 1) % lat_n, (lat + 1) % lat_n

    sum0, sum1 = [
        CoreSum((0, 1, 2), grads, got, halves, final, (core_send.at[k], core_recv.at[k]), terms, part, cross, sum_send.at[k], sum_recv.at[k])
        for k, (grads, got, halves, final, terms, part, cross) in enumerate((
            (grads0, got0, halves0, final0, terms0, part0, cross0), (grads1, got1, halves1, final1, terms1, part1, cross1),
        ))
    ]
    sum_t = PlaneSum((1, 2, 0), lambda p: grads_t.at[p], terms_t, part_t, cross_t, final_t, sum_send.at[2], sum_recv.at[2])

    barrier = pltpu.get_barrier_semaphore()
    partners = [(west, lat), (east, lat), (lon, above), (lon, below), (west, above), (east, below)]
    chip = list(place())
    lines = []
    for axis in range(3):
        for s in range(1, 4):
            at = list(chip)
            at[axis] = (at[axis] + s) % 4
            lines.append(device_at(*at))
    partners += [sum0.other] + lines
    for device in partners:
        pl.semaphore_signal(barrier, inc=1, device_id=device, device_id_type=MESH_ID)
    loads = [pltpu.make_async_copy(a, b, load_sems.at[k]) for k, (a, b) in enumerate(zip(sources, held))]
    first = (6, 9, 8, 10, 11)
    for k in first:
        loads[k].start()
    pl.semaphore_wait(barrier, len(partners))

    right, left = pl.ds(HALF, HALF), pl.ds(0, HALF)
    upper, lower = pl.ds(0, 3), pl.ds(3, 3)
    halos = []
    for k, source in enumerate((field_ref, cot_ref)):
        win = win_ref.at[k]
        copies = [pltpu.make_async_copy(source.at[lower, :, right], win.at[upper, :, left], local_sems.at[k])]
        for s, (rows, cols, device) in enumerate((((lower, upper), (left, right), (west, lat)), ((upper, lower), (right, left), (lon, above)), ((upper, lower), (left, right), (west, above)))):
            copies.append(remote(source.at[rows[0], :, cols[0]], win.at[rows[1], :, cols[1]], halo_send.at[3 * k + s], halo_recv.at[3 * k + s], device))
        halos.append(copies)
    for copy in halos[0]:
        copy.start()
    for k in range(len(loads)):
        if k not in first:
            loads[k].start()

    def trail(value, k, out):
        win = send_ref.at[k]
        back = nt(perm[...], value)
        for c in range(WC):
            win[:, :, c * C:(c + 1) * C] = back[c * 48:(c + 1) * 48].reshape(WR, 8, C).astype(BF)
        copies = [pltpu.make_async_copy(win.at[upper, :, left], out.at[lower, :, right], local_sems.at[2 + k])]
        for s, (rows, cols, device) in enumerate((((upper, lower), (right, left), (east, lat)), ((lower, upper), (left, right), (lon, below)), ((lower, upper), (right, left), (east, below)))):
            copies.append(remote(win.at[rows[0], :, cols[0]], out.at[rows[1], :, cols[1]], trail_send.at[3 * k + s], trail_recv.at[3 * k + s], device))
        for copy in copies:
            copy.start()
        return copies

    for k in first:
        loads[k].wait()
    for device in lines:
        pl.semaphore_signal(ready, inc=1, device_id=device, device_id_type=MESH_ID)

    t_ref[...] = jnp.zeros_like(t_ref)
    for w in range(NW):
        for h in range(HEADS):
            t_ref[h * RELP:h * RELP + REL, :] = table[w, h, :, 0, :]
        rest = t_ref[...]
        moved = []
        for part in range(3):
            low = rest.astype(BF)
            rest = rest - low.astype(F32)
            moved.append(nn(low, pair[...]).astype(BF))
        spread = tn(jnp.concatenate(moved, axis=0), rep[...])
        z = spread[0:16] * entry[0:1]
        for a in range(1, A):
            z = z + spread[16 * a:16 * a + 16] * entry[a:a + 1]
        hide = jnp.where(lat == lat_n - 1, differs[1], 0.0)
        if w == NW - 1:
            hide = hide + differs[0]
        z = jnp.where(hide > 0.5, MASKED, z)
        for cs in range(WC):
            for h in range(HEADS):
                at = h * REL * A + (11 - cs) * A
                bias_ref[w, cs * A:(cs + 1) * A, h * TW:(h + 1) * TW] = z[0:A, at:at + TW]

    qblk_ref[...] = jnp.zeros_like(qblk_ref)
    dblk_ref[...] = jnp.zeros_like(dblk_ref)

    for k in range(len(loads)):
        if k not in first:
            loads[k].wait()
    qkv_t[...] = qkv_w[...].T
    proj_t[...] = proj_w[...].T
    fc1_t[...] = fc1_w[...].T
    fc2_t[...] = fc2_w[...].T

    for copy in halos[0]:
        copy.wait()
    for copy in halos[1]:
        copy.start()
    field = tn(tokens_of(x_ref, win_ref.at[0]), perm[...])

    gain1 = column_of(gain_attn[...])
    gain2 = column_of(gain_mlp[...])
    hat1, inv1 = normalise(field)
    normed1 = (hat1 * gain1).astype(BF)
    projected = nn(qkv_t[...], normed1)
    scaling = HEAD ** (-0.5)
    q_ref[...] = (projected[0:C] * scaling).astype(BF)
    k_ref[...] = projected[C:2 * C].astype(BF)
    v_ref[...] = projected[2 * C:].astype(BF)
    kv_ref[...] = tn(normed1, qkv_w[:, C:]).astype(BF)
    blocks = [(slice(h * HEAD, (h + 1) * HEAD), slice(h * TW, (h + 1) * TW)) for h in range(HEADS)]

    for w in range(NW):
        rows = slice(w * TW, (w + 1) * TW)
        for head, cols in blocks:
            qblk_ref[w, head, cols] = q_ref[head, rows]
        scores = nn(kv_ref[rows, 0:C], qblk_ref[w]) + bias_ref[w]
        raised = jnp.exp(scores - jnp.max(scores, axis=0, keepdims=True))
        probs = raised * (1.0 / jnp.sum(raised, axis=0, keepdims=True))
        p_ref[w] = probs
        context = nn(v_ref[:, rows], probs.astype(BF)).astype(BF)
        for head, cols in blocks:
            ctx_ref[head, rows] = context[head, cols]
    attended = nn(proj_t[...], ctx_ref[...]).astype(BF)

    for copy in halos[1]:
        copy.wait()
    cot = tn(tokens_of(x_ref, win_ref.at[1]), perm[...])
    cot_low = cot.astype(BF)

    resid = field + attended.astype(F32)
    hat2, inv2 = normalise(resid)
    normed2 = (hat2 * gain2).astype(BF)
    hidden = nn(fc1_t[...], normed2)
    k0 = 0.7978845608028654
    k1 = 0.044715
    sq = hidden * hidden
    th = jnp.tanh(hidden * (k0 + (k0 * k1) * sq))
    half = 0.5 * (1.0 + th)
    act = (hidden * half).astype(BF)
    slope = half + 0.5 * hidden * (1.0 - th * th) * (k0 + (3.0 * k0 * k1) * sq)
    d_act = nn(fc2_t[...], cot_low).astype(BF)
    d_pre = (d_act.astype(F32) * slope).astype(BF)
    fc1_grad = nt(normed2, d_pre).astype(BF)
    fc2_grad = nt(cot_low, act).astype(BF)
    for k in range(6):
        put_tiles(grads0, ROWS[0], k * C, fc1_grad[:, k * LANES:(k + 1) * LANES])
        put_tiles(grads0, ROWS[0], (6 + k) * C, fc2_grad[:, k * LANES:(k + 1) * LANES])
    d_normed2 = nn(fc1_w[...], d_pre)
    gain2_grad = row_of(jnp.sum(d_normed2 * hat2, axis=1, keepdims=True))
    d_resid = cot + normalise_back(d_normed2 * gain2, hat2, inv2)
    d_att = d_resid.astype(BF)
    proj_grad = nt(ctx_ref[...], d_att).astype(BF)
    put_tiles(grads0, ROWS[0], 12 * C, proj_grad[:, C - LANES:])
    gain_rows = jnp.concatenate([gain2_grad[:, 0:LANES], gain2_grad[:, C - LANES:], jnp.zeros((62, LANES), F32)], axis=0)
    put_tiles(grads0, ROWS[0], 13 * C, gain_rows.astype(BF))
    sum0.start_core()
    mixed = (resid + nn(fc2_w[...], act)).astype(BF)
    mixed_copies = trail(mixed, 0, mixed_out)
    dctx_ref[...] = nn(proj_w[...], d_att).astype(BF)

    for w in range(NW):
        if w == 1:
            pl.semaphore_wait(ready, len(lines))
            sum0.start()
        rows = slice(w * TW, (w + 1) * TW)
        for head, cols in blocks:
            dblk_ref[w, head, cols] = dctx_ref[head, rows]
        dblk = dblk_ref[w]
        probs = p_ref[w]
        d_probs = nn(kv_ref[rows, C:], dblk)
        weighted = probs * d_probs
        d_scores = weighted - probs * jnp.sum(weighted, axis=0, keepdims=True)
        d_low = d_scores.astype(BF)
        dproj_ref[2 * C:, rows] = nt(dblk, probs.astype(BF)).astype(BF)
        dproj_ref[C:2 * C, rows] = nt(qblk_ref[w], d_low).astype(BF)
        d_q = (nn(k_ref[:, rows], d_low) * scaling).astype(BF)
        for head, cols in blocks:
            dproj_ref[head, rows] = d_q[head, cols]
        p_ref[w] = d_scores

    dproj = dproj_ref[...]
    qkv_grad = nt(normed1, dproj).astype(BF)
    d_win = nn(qkv_w[...], dproj).astype(BF).astype(F32)
    gain1_grad = row_of(jnp.sum(d_win * hat1, axis=1, keepdims=True))
    for k in range(4):
        put_tiles(grads1, ROWS[1], k * C, qkv_grad[:, k * LANES:(k + 1) * LANES])
    put_tiles(grads1, ROWS[1], 4 * C, jnp.concatenate([qkv_grad[:, 4 * LANES:], proj_grad[:, 0:64]], axis=1))
    gain_rows = jnp.concatenate([gain1_grad[:, 0:LANES], gain1_grad[:, C - LANES:], jnp.zeros((62, LANES), F32)], axis=0)
    put_tiles(grads1, ROWS[1], 5 * C, gain_rows.astype(BF))
    sum1.start_core()

    for w in range(NW):
        z_ref[...] = jnp.zeros_like(z_ref)
        for cs in range(WC):
            for h in range(HEADS):
                at = h * REL * A + (11 - cs) * A
                z_ref[0:A, at:at + TW] += p_ref[w, cs * A:(cs + 1) * A, h * TW:(h + 1) * TW]
        dz = z_ref[...]
        spread = jnp.concatenate([dz * entry[a:a + 1] for a in range(A)], axis=0).astype(BF)
        d_table = nt(nt(rep[0:HEADS * RELP, :], spread).astype(BF), pair[...]).astype(BF)
        for k in range(3):
            grads_t[3 * w + k] = d_table[TROWS * k:TROWS * (k + 1), 0:LANES]
            grads_t[12 + k, :, 16 * w:16 * w + 16] = d_table[TROWS * k:TROWS * (k + 1), LANES:]
        if w == 1:
            sum1.start()
    for k in range(3):
        grads_t[12 + k, :, 64:] = jnp.zeros((TROWS, 64), BF)
    grads_t[15] = jnp.zeros((TROWS, LANES), BF)
    sum_t.start()

    d_field = (d_resid + normalise_back(d_win * gain1, hat1, inv1)).astype(BF)
    sum0.across()
    sum1.across()
    fgrad_copies = trail(d_field, 1, fgrad_out)
    sum1.back()
    sum_t.across()
    sum0.back()
    sum_t.back()
    sum1.finish()
    sum0.finish()
    sum_t.finish()
    sum1.finish_core()
    sum0.finish_core()
    for each in (sum0, sum1, sum_t):
        each.finish_sends()
    for copy in mixed_copies + fgrad_copies:
        copy.wait()


def results_kernel(
    mixed_in, fgrad_in, final0, final1, final_t,
    mixed_out, fgrad_out, qkv_out, proj_out, fc1_out, fc2_out, gain_attn_out, gain_mlp_out, table_out,
    qkv, proj, fc1, fc2, gain_attn, gain_mlp, table, sems,
):
    outward = []

    def send(value, out):
        outward.append(pltpu.make_async_copy(value, out, sems.at[len(outward)]))
        outward[-1].start()

    send(mixed_in, mixed_out)
    send(fgrad_in, fgrad_out)
    for w in range(NW):
        wide = jnp.concatenate([final_t[3 * w + k].astype(F32) for k in range(3)], axis=0)
        tail = jnp.concatenate([final_t[12 + k].astype(F32) for k in range(3)], axis=0)
        for h in range(HEADS):
            table[w, h, :, 0, 0:LANES] = wide[h * RELP:h * RELP + REL]
            table[w, h, :, 0, LANES:] = tail[h * RELP:h * RELP + REL, 16 * w:16 * w + 16]
    send(table, table_out)
    for k in range(6):
        fc1[:, k * LANES:(k + 1) * LANES] = get_tiles(final0, ROWS[0], k * C, C)
    send(fc1, fc1_out)
    for k in range(6):
        fc2[:, k * LANES:(k + 1) * LANES] = get_tiles(final0, ROWS[0], (6 + k) * C, C)
    send(fc2, fc2_out)
    proj[:, 64:] = get_tiles(final0, ROWS[0], 12 * C, C)
    for k in range(4):
        qkv[:, k * LANES:(k + 1) * LANES] = get_tiles(final1, ROWS[1], k * C, C)
    shared = get_tiles(final1, ROWS[1], 4 * C, C)
    qkv[:, 4 * LANES:] = shared[:, 0:64]
    proj[:, 0:64] = shared[:, 64:]
    send(qkv, qkv_out)
    send(proj, proj_out)
    for gain, out, final, row in ((gain_attn, gain_attn_out, final1, 5 * C), (gain_mlp, gain_mlp_out, final0, 13 * C)):
        rows = get_tiles(final, final.shape[1], row, 16)
        gain[:, 0:LANES] = rows[0:1]
        gain[:, LANES:] = rows[1:2, 64:]
        send(gain, out)
    for copy in outward:
        copy.wait()


def shards(field, cotangent, gain_attn, gain_mlp, qkv_weight, proj_weight, fc1_weight, fc2_weight, bias_table):
    consts = [jnp.asarray(v) for v in constants()]
    sds = jax.ShapeDtypeStruct
    vm = pl.BlockSpec(memory_space=pltpu.VMEM)
    hbm = pl.BlockSpec(memory_space=pl.ANY)
    levels, rows, flat = field.shape
    tile = (rows, levels, flat)
    dma = pltpu.SemaphoreType.DMA
    operands = [
        field.transpose(1, 0, 2), cotangent.transpose(1, 0, 2), gain_attn.reshape(1, C), gain_mlp.reshape(1, C),
        qkv_weight, proj_weight, fc1_weight, fc2_weight.T, bias_table.transpose(0, 2, 3, 1, 4), *consts,
    ]
    pieces = pl.pallas_call(
        block_kernel,
        out_shape=(
            sds(tile, BF), sds(tile, BF),
            sds((2 * PEERS, ROWS[0], LANES), BF), sds((2 * PEERS, ROWS[1], LANES), BF), sds((PEERS, TROWS, LANES), BF),
        ),
        in_specs=[hbm] * len(operands),
        out_specs=(vm,) * 5,
        scratch_shapes=[pltpu.VMEM(v.shape, v.dtype) for v in operands[2:]] + [
            pltpu.VMEM((TOK, C), F32),
            pltpu.VMEM((HEADS * RELP, TW), F32),
            pltpu.VMEM((NW, TW, HT), F32),
            pltpu.VMEM((16, ZL), F32),
            pltpu.VMEM((NW, TW, HT), F32),
            pltpu.VMEM((NW, C, HT), BF), pltpu.VMEM((NW, C, HT), BF),
            pltpu.VMEM((C, TOK), BF), pltpu.VMEM((C, TOK), BF), pltpu.VMEM((C, TOK), BF),
            pltpu.VMEM((TOK, 2 * C), BF),
            pltpu.VMEM((C, TOK), BF), pltpu.VMEM((C, TOK), BF),
            pltpu.VMEM((3 * C, TOK), BF),
            pltpu.VMEM((3 * C, C), BF), pltpu.VMEM((C, C), BF), pltpu.VMEM((HID, C), BF), pltpu.VMEM((HID, C), BF),
            pltpu.VMEM((2,) + tile, BF),
            pltpu.VMEM((2,) + tile, BF),
            pltpu.VMEM((2 * PEERS, ROWS[0], LANES), BF), pltpu.VMEM((2 * PEERS, ROWS[1], LANES), BF), pltpu.VMEM((PEERS, TROWS, LANES), BF),
            pltpu.VMEM((PEERS, ROWS[0], LANES), BF), pltpu.VMEM((PEERS, ROWS[1], LANES), BF),
            pltpu.VMEM((PEERS, ROWS[0], LANES), BF), pltpu.VMEM((PEERS, ROWS[1], LANES), BF),
            pltpu.VMEM((PEERS, ROWS[0], LANES), BF), pltpu.VMEM((PEERS, ROWS[1], LANES), BF), pltpu.VMEM((PEERS, TROWS, LANES), BF),
            pltpu.VMEM((2, ROWS[0], LANES), BF), pltpu.VMEM((2, ROWS[1], LANES), BF), pltpu.VMEM((2, TROWS, LANES), BF),
            pltpu.VMEM((4, ROWS[0], LANES), BF), pltpu.VMEM((4, ROWS[1], LANES), BF), pltpu.VMEM((2, TROWS, LANES), BF),
            dma((len(operands) - 2,)), dma((7,)), dma((6,)), dma((6,)), dma((6,)), dma((6,)), dma((2, 2)), dma((2, 2)),
            dma((3, 3)), dma((3, 3)), pltpu.SemaphoreType.REGULAR,
        ],
        compiler_params=pltpu.CompilerParams(vmem_limit_bytes=36 * 1024 * 1024, collective_id=0, has_side_effects=True),
        name="block",
    )(
        *[pltpu.with_memory_space_constraint(v, pltpu.HBM) for v in operands]
    )
    shapes = [(C, 3 * C), (C, C), (C, HID), (C, HID), (1, C), (1, C), (NW, HEADS, REL, 1, TW)]
    mixed, fgrad, qkv, proj, fc1, fc2, gain1, gain2, table = pl.pallas_call(
        results_kernel,
        out_shape=[sds(tile, BF)] * 2 + [sds(v, F32) for v in shapes],
        in_specs=[vm] * 5,
        out_specs=[hbm] * 9,
        scratch_shapes=[pltpu.VMEM(v, F32) for v in shapes] + [dma((9,))],
        compiler_params=pltpu.CompilerParams(vmem_limit_bytes=16 * 1024 * 1024),
        name="results",
    )(*pieces)
    return (
        mixed.transpose(1, 0, 2), fgrad.transpose(1, 0, 2), qkv, proj, fc1, fc2.T,
        gain1.reshape(C), gain2.reshape(C), table.transpose(0, 3, 1, 2, 4),
    )


def solution(mesh):
    grid = P(None, "lat", "lon")
    by_type = P(None, "lat", None, None, None)
    return jax.shard_map(
        shards,
        mesh=mesh,
        in_specs=(grid, grid) + (P(),) * 6 + (by_type,),
        out_specs=(grid, grid) + (P(),) * 6 + (by_type,),
        check_vma=False,
    )
```

```python
import functools
import jax
import jax.numpy as jnp
import numpy as np
from jax import lax
from jax.experimental import pallas as pl
from jax.experimental.pallas import tpu as pltpu
from jax.sharding import PartitionSpec as P

BF = jnp.bfloat16
F32 = jnp.float32
C = 192
HEADS = 6
HEAD = 32
HID = 768
WZ, WR, WC = 2, 6, 12
A = WZ * WR
TW = A * WC
NW = 4
TOK = NW * TW
REL = 2 * WC - 1
RELP = 24
HT = HEADS * TW
ZL = REL * HEADS * A
EPS = 1e-05
MASKED = -1000000000.0


def constants():
    perm = np.zeros((WC, WR, 8, NW, WC, WZ, WR), np.float32)
    for c in range(WC):
        for w in range(NW):
            for lev in range(WZ):
                for r in range(WR):
                    perm[c, r, (2 * w + lev + 1) % 8, w, c, lev, r] = 1
    perm = perm.reshape(TOK, TOK)
    rep = np.zeros((HEADS, RELP, HEADS, REL, A), np.float32)
    for h in range(HEADS):
        for rel in range(REL):
            rep[h, rel, h, rel, :] = 1
    rep = np.concatenate([rep.reshape(HEADS * RELP, ZL)] * 3)
    pair = np.zeros((WZ, WZ, WR, WR, WZ, WR, 16), np.float32)
    for lt in range(WZ):
        for ls in range(WZ):
            for rt in range(WR):
                for rs in range(WR):
                    pair[lt, ls, rt, rs, lt, rt, ls * WR + rs] = 1
    pair = pair.reshape(TW, A * 16)
    lane_a = np.arange(ZL) % A
    entry = (np.arange(A)[:, None] == lane_a[None, :]).astype(np.float32)
    entry = np.concatenate([entry, np.zeros((4, ZL), np.float32)])
    b = np.arange(16)
    level_differs = ((b[:, None] // WR) != (lane_a[None, :] // WR)) & (b[:, None] < A)
    row_differs = ((b[:, None] % WR >= 3) != (lane_a[None, :] % WR >= 3)) & (b[:, None] < A)
    differs = np.stack([level_differs, row_differs]).astype(np.float32)
    return [np.asarray(v, dtype=BF) for v in (perm, rep, pair)] + [entry, differs]


def nn(a, b):
    return lax.dot_general(a, b, (((1,), (0,)), ((), ())), preferred_element_type=F32)


def nt(a, b):
    return lax.dot_general(a, b, (((1,), (1,)), ((), ())), preferred_element_type=F32)


def tn(a, b):
    return lax.dot_general(a, b, (((0,), (0,)), ((), ())), preferred_element_type=F32)


def column_of(row):
    size = row.shape[1]
    eye = lax.broadcasted_iota(jnp.int32, (size, size), 0) == lax.broadcasted_iota(jnp.int32, (size, size), 1)
    return jnp.sum(jnp.where(eye, row, 0.0), axis=1, keepdims=True)


def row_of(column):
    size = column.shape[0]
    eye = lax.broadcasted_iota(jnp.int32, (size, size), 0) == lax.broadcasted_iota(jnp.int32, (size, size), 1)
    return jnp.sum(jnp.where(eye, column, 0.0), axis=0, keepdims=True)


def normalise(v):
    centre = v - jnp.sum(v, axis=0, keepdims=True) * (1.0 / C)
    inv = lax.rsqrt(jnp.sum(centre * centre, axis=0, keepdims=True) * (1.0 / C) + EPS)
    return centre * inv, inv


def normalise_back(g, hat, inv):
    return inv * (g - jnp.sum(g, axis=0, keepdims=True) * (1.0 / C) - hat * (jnp.sum(g * hat, axis=0, keepdims=True) * (1.0 / C)))


def tokens_of(x_ref, win):
    for c in range(WC):
        x_ref[c * 48:(c + 1) * 48, :] = win[:, :, c * C:(c + 1) * C].astype(F32).reshape(48, C)
    return x_ref[...].astype(BF)


HALF = WC * C // 2
LANES = 128
PEERS = 16
ROWS = (80, 32)
TROWS = 48
MESH_ID = pl.DeviceIdType.MESH
FARTHEST_FIRST = sorted(range(1, PEERS), key=lambda s: -sum(min(far, 4 - far) for far in divmod(s, 4)))


def place():
    lon, lat = lax.axis_index("lon"), lax.axis_index("lat")
    return (lon // 4) % 2 * 2 + lat // 2, lon // 8, lon % 4, lat % 2


def device_at(x, y, z, core):
    return ((y * 2 + x // 2) * 4 + z, x % 2 * 2 + core)


def remote(src, dst, send_sem, recv_sem, device):
    return pltpu.make_async_remote_copy(
        src_ref=src, dst_ref=dst, send_sem=send_sem, recv_sem=recv_sem, device_id=device, device_id_type=MESH_ID
    )


def drain(like, sem):
    pltpu.make_async_copy(like, like, sem).wait()


def total(ref, count):
    value = ref[0].astype(F32)
    for k in range(1, count):
        value = value + ref[k].astype(F32)
    return value.astype(BF)


class PlaneSum:
    def __init__(self, axes, piece, terms, part, cross, final, sends, recvs):
        self.axes, self.piece, self.terms, self.part, self.cross, self.final = axes, piece, terms, part, cross, final
        self.sends, self.recvs = sends, recvs
        self.at = place()
        self.me = self.at[axes[0]] * 4 + self.at[axes[1]]
        self.count = cross.shape[0]
        self.step = 4 // self.count
        self.mine = self.at[axes[2]] // self.step
        self.others = terms.at[pl.ds(1, PEERS - 1)]
        self.few = cross.at[pl.ds(1, self.count - 1)]

    def in_plane(self, s):
        at = list(self.at)
        for axis, far in zip(self.axes, divmod(s, 4)):
            at[axis] = (at[axis] + far) % 4
        return at[self.axes[0]] * 4 + at[self.axes[1]], device_at(*at)

    def along(self, s):
        at = list(self.at)
        at[self.axes[2]] = (at[self.axes[2]] + s * self.step) % 4
        return device_at(*at)

    def start(self):
        for s in FARTHEST_FIRST:
            p, device = self.in_plane(s)
            remote(self.piece(p), self.terms.at[s], self.sends.at[0], self.recvs.at[0], device).start()

    def across(self):
        self.terms[0] = self.piece(self.me)[...]
        drain(self.others, self.recvs.at[0])
        value = total(self.terms, PEERS)
        self.part[0] = value
        self.cross[self.mine] = value
        for s in range(1, self.count):
            remote(self.part.at[0], self.cross.at[self.mine], self.sends.at[1], self.recvs.at[1], self.along(s)).start()

    def back(self):
        drain(self.few, self.recvs.at[1])
        value = total(self.cross, self.count)
        self.part[1] = value
        self.final[self.first + self.me] = value
        for s in FARTHEST_FIRST:
            remote(self.part.at[1], self.final.at[self.first + self.me], self.sends.at[2], self.recvs.at[2], self.in_plane(s)[1]).start()

    def finish(self):
        drain(self.others, self.recvs.at[2])

    def finish_sends(self):
        drain(self.others, self.sends.at[0])
        drain(self.few, self.sends.at[1])
        drain(self.others, self.sends.at[2])

    first = 0


class CoreSum(PlaneSum):
    def __init__(self, axes, grads, got, halves, final, core_sems, *args):
        self.grads, self.got, self.halves, self.core_sems = grads, got, halves, core_sems
        super().__init__(axes, lambda p: halves.at[p], *args[:3], final, *args[3:])
        self.core = self.at[3]
        self.first = self.core * PEERS
        self.other = device_at(*self.at[:3], 1 - self.core)

    def start_core(self):
        self.swap = remote(self.grads.at[pl.ds((1 - self.core) * PEERS, PEERS)], self.got, self.core_sems[0].at[0], self.core_sems[1].at[0], self.other)
        self.swap.start()

    def start(self):
        self.swap.wait()
        for p in range(PEERS):
            self.halves[p] = (self.grads[self.core * PEERS + p].astype(F32) + self.got[p].astype(F32)).astype(BF)
        super().start()

    def finish(self):
        super().finish()
        mine = self.final.at[pl.ds(self.first, PEERS)]
        self.swap = remote(mine, mine, self.core_sems[0].at[1], self.core_sems[1].at[1], self.other)
        self.swap.start()

    def finish_core(self):
        self.swap.wait()


def put_tiles(ref, rows, first, value):
    done = 0
    while done < value.shape[0]:
        piece, row = divmod(first + done, rows)
        count = min(rows - row, value.shape[0] - done)
        ref[piece, row:row + count, :] = value[done:done + count]
        done += count


def get_tiles(ref, rows, first, count):
    parts, done = [], 0
    while done < count:
        piece, row = divmod(first + done, rows)
        take = min(rows - row, count - done)
        parts.append(ref[piece, row:row + take, :].astype(F32))
        done += take
    return parts[0] if len(parts) == 1 else jnp.concatenate(parts, axis=0)


def block_kernel(
    field_ref, cot_ref, *refs,
):
    count = 12
    sources, outs, (held, rest) = refs[:count], refs[count:count + 5], (refs[count + 5:2 * count + 5], refs[2 * count + 5:])
    block(field_ref, cot_ref, sources, held, *outs, *rest)


def block(
    field_ref, cot_ref, sources, held,
    mixed_out, fgrad_out, final0, final1, final_t,
    x_ref, t_ref, bias_ref, z_ref, p_ref, qblk_ref, dblk_ref, q_ref, k_ref, v_ref, kv_ref, ctx_ref, dctx_ref, dproj_ref, qkv_t, proj_t, fc1_t, fc2_t,
    win_ref, send_ref, grads0, grads1, grads_t, got0, got1, halves0, halves1,
    terms0, terms1, terms_t, part0, part1, part_t, cross0, cross1, cross_t,
    load_sems, local_sems, halo_send, halo_recv, trail_send, trail_recv, core_send, core_recv,
    sum_send, sum_recv, ready,
):
    gain_attn, gain_mlp, qkv_w, proj_w, fc1_w, fc2_w, table, perm, rep, pair, entry, differs = held
    lon, lat = lax.axis_index("lon"), lax.axis_index("lat")
    lon_n, lat_n = 32, 4
    west, east = (lon + lon_n - 1) % lon_n, (lon + 1) % lon_n
    above, below = (lat + lat_n - 1) % lat_n, (lat + 1) % lat_n

    sum0, sum1 = [
        CoreSum((0, 1, 2) if k == 0 else (0, 2, 1), grads, got, halves, final, (core_send.at[k], core_recv.at[k]), terms, part, cross, sum_send.at[k], sum_recv.at[k])
        for k, (grads, got, halves, final, terms, part, cross) in enumerate((
            (grads0, got0, halves0, final0, terms0, part0, cross0), (grads1, got1, halves1, final1, terms1, part1, cross1),
        ))
    ]
    sum_t = PlaneSum((1, 2, 0), lambda p: grads_t.at[p], terms_t, part_t, cross_t, final_t, sum_send.at[2], sum_recv.at[2])

    barrier = pltpu.get_barrier_semaphore()
    partners = [(west, lat), (east, lat), (lon, above), (lon, below), (west, above), (east, below)]
    chip = list(place())
    lines = []
    for axis in range(3):
        for s in range(1, 4):
            at = list(chip)
            at[axis] = (at[axis] + s) % 4
            lines.append(device_at(*at))
    partners += [sum0.other] + lines
    for device in partners:
        pl.semaphore_signal(barrier, inc=1, device_id=device, device_id_type=MESH_ID)
    loads = [pltpu.make_async_copy(a, b, load_sems.at[k]) for k, (a, b) in enumerate(zip(sources, held))]
    first = (6, 9, 8, 10, 11)
    for k in first:
        loads[k].start()
    pl.semaphore_wait(barrier, len(partners))

    right, left = pl.ds(HALF, HALF), pl.ds(0, HALF)
    upper, lower = pl.ds(0, 3), pl.ds(3, 3)
    halos = []
    for k, source in enumerate((field_ref, cot_ref)):
        win = win_ref.at[k]
        copies = [pltpu.make_async_copy(source.at[lower, :, right], win.at[upper, :, left], local_sems.at[k])]
        for s, (rows, cols, device) in enumerate((((lower, upper), (left, right), (west, lat)), ((upper, lower), (right, left), (lon, above)), ((upper, lower), (left, right), (west, above)))):
            copies.append(remote(source.at[rows[0], :, cols[0]], win.at[rows[1], :, cols[1]], halo_send.at[3 * k + s], halo_recv.at[3 * k + s], device))
        halos.append(copies)
    for copy in halos[0]:
        copy.start()
    for k in range(len(loads)):
        if k not in first:
            loads[k].start()

    def trail(value, k, out):
        win = send_ref.at[k]
        back = nt(perm[...], value)
        for c in range(WC):
            win[:, :, c * C:(c + 1) * C] = back[c * 48:(c + 1) * 48].reshape(WR, 8, C).astype(BF)
        copies = [pltpu.make_async_copy(win.at[upper, :, left], out.at[lower, :, right], local_sems.at[2 + k])]
        for s, (rows, cols, device) in enumerate((((upper, lower), (right, left), (east, lat)), ((lower, upper), (left, right), (lon, below)), ((lower, upper), (right, left), (east, below)))):
            copies.append(remote(win.at[rows[0], :, cols[0]], out.at[rows[1], :, cols[1]], trail_send.at[3 * k + s], trail_recv.at[3 * k + s], device))
        for copy in copies:
            copy.start()
        return copies

    for k in first:
        loads[k].wait()
    for device in lines:
        pl.semaphore_signal(ready, inc=1, device_id=device, device_id_type=MESH_ID)

    t_ref[...] = jnp.zeros_like(t_ref)
    for w in range(NW):
        for h in range(HEADS):
            t_ref[h * RELP:h * RELP + REL, :] = table[w, h, :, 0, :]
        rest = t_ref[...]
        moved = []
        for part in range(3):
            low = rest.astype(BF)
            rest = rest - low.astype(F32)
            moved.append(nn(low, pair[...]).astype(BF))
        spread = tn(jnp.concatenate(moved, axis=0), rep[...])
        z = spread[0:16] * entry[0:1]
        for a in range(1, A):
            z = z + spread[16 * a:16 * a + 16] * entry[a:a + 1]
        hide = jnp.where(lat == lat_n - 1, differs[1], 0.0)
        if w == NW - 1:
            hide = hide + differs[0]
        z = jnp.where(hide > 0.5, MASKED, z)
        for cs in range(WC):
            for h in range(HEADS):
                at = h * REL * A + (11 - cs) * A
                bias_ref[w, cs * A:(cs + 1) * A, h * TW:(h + 1) * TW] = z[0:A, at:at + TW]

    qblk_ref[...] = jnp.zeros_like(qblk_ref)
    dblk_ref[...] = jnp.zeros_like(dblk_ref)

    for k in range(len(loads)):
        if k not in first:
            loads[k].wait()
    qkv_t[...] = qkv_w[...].T
    proj_t[...] = proj_w[...].T
    fc1_t[...] = fc1_w[...].T
    fc2_t[...] = fc2_w[...].T

    for copy in halos[0]:
        copy.wait()
    for copy in halos[1]:
        copy.start()
    field = tn(tokens_of(x_ref, win_ref.at[0]), perm[...])

    gain1 = column_of(gain_attn[...])
    gain2 = column_of(gain_mlp[...])
    hat1, inv1 = normalise(field)
    normed1 = (hat1 * gain1).astype(BF)
    projected = nn(qkv_t[...], normed1)
    scaling = HEAD ** (-0.5)
    q_ref[...] = (projected[0:C] * scaling).astype(BF)
    k_ref[...] = projected[C:2 * C].astype(BF)
    v_ref[...] = projected[2 * C:].astype(BF)
    kv_ref[...] = tn(normed1, qkv_w[:, C:]).astype(BF)
    blocks = [(slice(h * HEAD, (h + 1) * HEAD), slice(h * TW, (h + 1) * TW)) for h in range(HEADS)]

    for w in range(NW):
        rows = slice(w * TW, (w + 1) * TW)
        for head, cols in blocks:
            qblk_ref[w, head, cols] = q_ref[head, rows]
        scores = nn(kv_ref[rows, 0:C], qblk_ref[w]) + bias_ref[w]
        raised = jnp.exp(scores - jnp.max(scores, axis=0, keepdims=True))
        probs = raised * (1.0 / jnp.sum(raised, axis=0, keepdims=True))
        p_ref[w] = probs
        context = nn(v_ref[:, rows], probs.astype(BF)).astype(BF)
        for head, cols in blocks:
            ctx_ref[head, rows] = context[head, cols]
    attended = nn(proj_t[...], ctx_ref[...]).astype(BF)

    for copy in halos[1]:
        copy.wait()
    cot = tn(tokens_of(x_ref, win_ref.at[1]), perm[...])
    cot_low = cot.astype(BF)

    resid = field + attended.astype(F32)
    hat2, inv2 = normalise(resid)
    normed2 = (hat2 * gain2).astype(BF)
    hidden = nn(fc1_t[...], normed2)
    k0 = 0.7978845608028654
    k1 = 0.044715
    sq = hidden * hidden
    th = jnp.tanh(hidden * (k0 + (k0 * k1) * sq))
    half = 0.5 * (1.0 + th)
    act = (hidden * half).astype(BF)
    slope = half + 0.5 * hidden * (1.0 - th * th) * (k0 + (3.0 * k0 * k1) * sq)
    d_act = nn(fc2_t[...], cot_low).astype(BF)
    d_pre = (d_act.astype(F32) * slope).astype(BF)
    fc1_grad = nt(normed2, d_pre).astype(BF)
    fc2_grad = nt(cot_low, act).astype(BF)
    for k in range(6):
        put_tiles(grads0, ROWS[0], k * C, fc1_grad[:, k * LANES:(k + 1) * LANES])
        put_tiles(grads0, ROWS[0], (6 + k) * C, fc2_grad[:, k * LANES:(k + 1) * LANES])
    d_normed2 = nn(fc1_w[...], d_pre)
    gain2_grad = row_of(jnp.sum(d_normed2 * hat2, axis=1, keepdims=True))
    d_resid = cot + normalise_back(d_normed2 * gain2, hat2, inv2)
    d_att = d_resid.astype(BF)
    proj_grad = nt(ctx_ref[...], d_att).astype(BF)
    put_tiles(grads0, ROWS[0], 12 * C, proj_grad[:, C - LANES:])
    gain_rows = jnp.concatenate([gain2_grad[:, 0:LANES], gain2_grad[:, C - LANES:], jnp.zeros((62, LANES), F32)], axis=0)
    put_tiles(grads0, ROWS[0], 13 * C, gain_rows.astype(BF))
    sum0.start_core()
    mixed = (resid + nn(fc2_w[...], act)).astype(BF)
    mixed_copies = trail(mixed, 0, mixed_out)
    dctx_ref[...] = nn(proj_w[...], d_att).astype(BF)

    for w in range(NW):
        if w == 1:
            pl.semaphore_wait(ready, len(lines))
            sum0.start()
        rows = slice(w * TW, (w + 1) * TW)
        for head, cols in blocks:
            dblk_ref[w, head, cols] = dctx_ref[head, rows]
        dblk = dblk_ref[w]
        probs = p_ref[w]
        d_probs = nn(kv_ref[rows, C:], dblk)
        weighted = probs * d_probs
        d_scores = weighted - probs * jnp.sum(weighted, axis=0, keepdims=True)
        d_low = d_scores.astype(BF)
        dproj_ref[2 * C:, rows] = nt(dblk, probs.astype(BF)).astype(BF)
        dproj_ref[C:2 * C, rows] = nt(qblk_ref[w], d_low).astype(BF)
        d_q = (nn(k_ref[:, rows], d_low) * scaling).astype(BF)
        for head, cols in blocks:
            dproj_ref[head, rows] = d_q[head, cols]
        p_ref[w] = d_scores

    dproj = dproj_ref[...]
    qkv_grad = nt(normed1, dproj).astype(BF)
    d_win = nn(qkv_w[...], dproj).astype(BF).astype(F32)
    gain1_grad = row_of(jnp.sum(d_win * hat1, axis=1, keepdims=True))
    for k in range(4):
        put_tiles(grads1, ROWS[1], k * C, qkv_grad[:, k * LANES:(k + 1) * LANES])
    put_tiles(grads1, ROWS[1], 4 * C, jnp.concatenate([qkv_grad[:, 4 * LANES:], proj_grad[:, 0:64]], axis=1))
    gain_rows = jnp.concatenate([gain1_grad[:, 0:LANES], gain1_grad[:, C - LANES:], jnp.zeros((62, LANES), F32)], axis=0)
    put_tiles(grads1, ROWS[1], 5 * C, gain_rows.astype(BF))
    sum1.start_core()

    for w in range(NW):
        z_ref[...] = jnp.zeros_like(z_ref)
        for cs in range(WC):
            for h in range(HEADS):
                at = h * REL * A + (11 - cs) * A
                z_ref[0:A, at:at + TW] += p_ref[w, cs * A:(cs + 1) * A, h * TW:(h + 1) * TW]
        dz = z_ref[...]
        spread = jnp.concatenate([dz * entry[a:a + 1] for a in range(A)], axis=0).astype(BF)
        d_table = nt(nt(rep[0:HEADS * RELP, :], spread).astype(BF), pair[...]).astype(BF)
        for k in range(3):
            grads_t[3 * w + k] = d_table[TROWS * k:TROWS * (k + 1), 0:LANES]
            grads_t[12 + k, :, 16 * w:16 * w + 16] = d_table[TROWS * k:TROWS * (k + 1), LANES:]
        if w == 1:
            sum1.start()
    for k in range(3):
        grads_t[12 + k, :, 64:] = jnp.zeros((TROWS, 64), BF)
    grads_t[15] = jnp.zeros((TROWS, LANES), BF)
    sum_t.start()

    d_field = (d_resid + normalise_back(d_win * gain1, hat1, inv1)).astype(BF)
    sum0.across()
    sum1.across()
    fgrad_copies = trail(d_field, 1, fgrad_out)
    sum_t.across()
    sum1.back()
    sum0.back()
    sum_t.back()
    sum1.finish()
    sum0.finish()
    sum_t.finish()
    sum1.finish_core()
    sum0.finish_core()
    for each in (sum0, sum1, sum_t):
        each.finish_sends()
    for copy in mixed_copies + fgrad_copies:
        copy.wait()


def results_kernel(
    mixed_in, fgrad_in, final0, final1, final_t,
    mixed_out, fgrad_out, qkv_out, proj_out, fc1_out, fc2_out, gain_attn_out, gain_mlp_out, table_out,
    qkv, proj, fc1, fc2, gain_attn, gain_mlp, table, sems,
):
    outward = []

    def send(value, out):
        outward.append(pltpu.make_async_copy(value, out, sems.at[len(outward)]))
        outward[-1].start()

    send(mixed_in, mixed_out)
    send(fgrad_in, fgrad_out)
    for w in range(NW):
        wide = jnp.concatenate([final_t[3 * w + k].astype(F32) for k in range(3)], axis=0)
        tail = jnp.concatenate([final_t[12 + k].astype(F32) for k in range(3)], axis=0)
        for h in range(HEADS):
            table[w, h, :, 0, 0:LANES] = wide[h * RELP:h * RELP + REL]
            table[w, h, :, 0, LANES:] = tail[h * RELP:h * RELP + REL, 16 * w:16 * w + 16]
    send(table, table_out)
    for k in range(6):
        fc1[:, k * LANES:(k + 1) * LANES] = get_tiles(final0, ROWS[0], k * C, C)
    send(fc1, fc1_out)
    for k in range(6):
        fc2[:, k * LANES:(k + 1) * LANES] = get_tiles(final0, ROWS[0], (6 + k) * C, C)
    send(fc2, fc2_out)
    proj[:, 64:] = get_tiles(final0, ROWS[0], 12 * C, C)
    for k in range(4):
        qkv[:, k * LANES:(k + 1) * LANES] = get_tiles(final1, ROWS[1], k * C, C)
    shared = get_tiles(final1, ROWS[1], 4 * C, C)
    qkv[:, 4 * LANES:] = shared[:, 0:64]
    proj[:, 0:64] = shared[:, 64:]
    send(qkv, qkv_out)
    send(proj, proj_out)
    for gain, out, final, row in ((gain_attn, gain_attn_out, final1, 5 * C), (gain_mlp, gain_mlp_out, final0, 13 * C)):
        rows = get_tiles(final, final.shape[1], row, 16)
        gain[:, 0:LANES] = rows[0:1]
        gain[:, LANES:] = rows[1:2, 64:]
        send(gain, out)
    for copy in outward:
        copy.wait()


def shards(field, cotangent, gain_attn, gain_mlp, qkv_weight, proj_weight, fc1_weight, fc2_weight, bias_table):
    consts = [jnp.asarray(v) for v in constants()]
    sds = jax.ShapeDtypeStruct
    vm = pl.BlockSpec(memory_space=pltpu.VMEM)
    hbm = pl.BlockSpec(memory_space=pl.ANY)
    levels, rows, flat = field.shape
    tile = (rows, levels, flat)
    dma = pltpu.SemaphoreType.DMA
    operands = [
        field.transpose(1, 0, 2), cotangent.transpose(1, 0, 2), gain_attn.reshape(1, C), gain_mlp.reshape(1, C),
        qkv_weight, proj_weight, fc1_weight, fc2_weight.T, bias_table.transpose(0, 2, 3, 1, 4), *consts,
    ]
    pieces = pl.pallas_call(
        block_kernel,
        out_shape=(
            sds(tile, BF), sds(tile, BF),
            sds((2 * PEERS, ROWS[0], LANES), BF), sds((2 * PEERS, ROWS[1], LANES), BF), sds((PEERS, TROWS, LANES), BF),
        ),
        in_specs=[hbm] * len(operands),
        out_specs=(vm,) * 5,
        scratch_shapes=[pltpu.VMEM(v.shape, v.dtype) for v in operands[2:]] + [
            pltpu.VMEM((TOK, C), F32),
            pltpu.VMEM((HEADS * RELP, TW), F32),
            pltpu.VMEM((NW, TW, HT), F32),
            pltpu.VMEM((16, ZL), F32),
            pltpu.VMEM((NW, TW, HT), F32),
            pltpu.VMEM((NW, C, HT), BF), pltpu.VMEM((NW, C, HT), BF),
            pltpu.VMEM((C, TOK), BF), pltpu.VMEM((C, TOK), BF), pltpu.VMEM((C, TOK), BF),
            pltpu.VMEM((TOK, 2 * C), BF),
            pltpu.VMEM((C, TOK), BF), pltpu.VMEM((C, TOK), BF),
            pltpu.VMEM((3 * C, TOK), BF),
            pltpu.VMEM((3 * C, C), BF), pltpu.VMEM((C, C), BF), pltpu.VMEM((HID, C), BF), pltpu.VMEM((HID, C), BF),
            pltpu.VMEM((2,) + tile, BF),
            pltpu.VMEM((2,) + tile, BF),
            pltpu.VMEM((2 * PEERS, ROWS[0], LANES), BF), pltpu.VMEM((2 * PEERS, ROWS[1], LANES), BF), pltpu.VMEM((PEERS, TROWS, LANES), BF),
            pltpu.VMEM((PEERS, ROWS[0], LANES), BF), pltpu.VMEM((PEERS, ROWS[1], LANES), BF),
            pltpu.VMEM((PEERS, ROWS[0], LANES), BF), pltpu.VMEM((PEERS, ROWS[1], LANES), BF),
            pltpu.VMEM((PEERS, ROWS[0], LANES), BF), pltpu.VMEM((PEERS, ROWS[1], LANES), BF), pltpu.VMEM((PEERS, TROWS, LANES), BF),
            pltpu.VMEM((2, ROWS[0], LANES), BF), pltpu.VMEM((2, ROWS[1], LANES), BF), pltpu.VMEM((2, TROWS, LANES), BF),
            pltpu.VMEM((4, ROWS[0], LANES), BF), pltpu.VMEM((4, ROWS[1], LANES), BF), pltpu.VMEM((2, TROWS, LANES), BF),
            dma((len(operands) - 2,)), dma((7,)), dma((6,)), dma((6,)), dma((6,)), dma((6,)), dma((2, 2)), dma((2, 2)),
            dma((3, 3)), dma((3, 3)), pltpu.SemaphoreType.REGULAR,
        ],
        compiler_params=pltpu.CompilerParams(vmem_limit_bytes=36 * 1024 * 1024, collective_id=0, has_side_effects=True),
        name="block",
    )(
        *[pltpu.with_memory_space_constraint(v, pltpu.HBM) for v in operands]
    )
    shapes = [(C, 3 * C), (C, C), (C, HID), (C, HID), (1, C), (1, C), (NW, HEADS, REL, 1, TW)]
    mixed, fgrad, qkv, proj, fc1, fc2, gain1, gain2, table = pl.pallas_call(
        results_kernel,
        out_shape=[sds(tile, BF)] * 2 + [sds(v, F32) for v in shapes],
        in_specs=[vm] * 5,
        out_specs=[hbm] * 9,
        scratch_shapes=[pltpu.VMEM(v, F32) for v in shapes] + [dma((9,))],
        compiler_params=pltpu.CompilerParams(vmem_limit_bytes=16 * 1024 * 1024),
        name="results",
    )(*pieces)
    return (
        mixed.transpose(1, 0, 2), fgrad.transpose(1, 0, 2), qkv, proj, fc1, fc2.T,
        gain1.reshape(C), gain2.reshape(C), table.transpose(0, 3, 1, 2, 4),
    )


def solution(mesh):
    grid = P(None, "lat", "lon")
    by_type = P(None, "lat", None, None, None)
    return jax.shard_map(
        shards,
        mesh=mesh,
        in_specs=(grid, grid) + (P(),) * 6 + (by_type,),
        out_specs=(grid, grid) + (P(),) * 6 + (by_type,),
        check_vma=False,
    )
```
